32 devices in a mesh: grp: 2 (over core), dev: 16 (over z, y, x).
Axes of the slice: x: 2, y: 2, z: 4, core: 2. Of those that a mesh axis runs over, the one named last changes fastest.
Arguments:
- forcing: float32 [4, 8, 256, 256], P(None, 'grp', 'dev'), may hold values from -6 to 6
- viscosity: float32 [8, 256, 256], P('grp', 'dev'), may hold values from 0.0316 to 31.6
Outputs:
- solution: float32 [4, 8, 256, 256], P(None, 'grp', 'dev')
- final_residual: float32 [4, 8, 256, 256], P(None, 'grp', 'dev')
The draws below stay inside these ranges and needn't reach their ends.
All inputs are finite; a program needn't handle non-finite values.
Results may differ from the reference program's by a relative error of at most 0.00002.
Values sent between devices are 32-bit elements; how exact they have to be, the bound alone decides.
A program may use at most 64 MiB of HBM per device.

```python
import math
import jax
import jax.numpy as jnp

NZ = 256
NU = 2
COARSE = 6
NX = 8
NY = 256


def shard_levels(own_key, shape, cuts, least, largest):
    def one(dim, blocks):
        steps = jax.random.uniform(jax.random.fold_in(jax.random.fold_in(own_key, 6), dim), (blocks,), jnp.float32, least / len(cuts), largest / len(cuts))
        return jnp.repeat(jnp.exp(steps), shape[dim] // blocks).reshape((-1,) + (1,) * (len(shape) - dim - 1))

    level = one(*cuts[0])
    for cut in cuts[1:]:
        level = level * one(*cut)
    return level


def gaussian(own_key, shape, deviation, most, shards=(), held_as=jnp.bfloat16):
    factor_of = shard_levels(own_key, shape, shards, -0.22, 0.18) if shards else 1.0
    drawn = jax.random.normal(own_key, shape, jnp.float32) * deviation * factor_of
    return jnp.minimum(jnp.maximum(drawn, -most), most).astype(held_as)


def setup_inputs(seed: int = 0) -> dict:
    arg_keys = jax.random.split(jax.random.key(seed), 3)
    forcing = gaussian(arg_keys[0], (4, NX, NY, NZ), 1.0, 6.0, ((1, 2), (2, 16)), jnp.float32)
    viscosity = jnp.clip(jnp.exp(math.log(31.6) - 6.9077553 * jax.random.uniform(arg_keys[1], (NX, NY, NZ), jnp.float32) ** shard_levels(arg_keys[1], (NX, NY, NZ), ((0, 2), (1, 16)), -0.2, 0.2)), 0.0316, 31.6)
    return dict(forcing=forcing, viscosity=viscosity)


OMEGA = 0.6
BETA = 0.25


def zero_pad(array):
    return jnp.pad(array, ((0, 0), (1, 1), (1, 1), (1, 1)))


def neighbours_of(padded):
    return [padded[:, 2:, 1:-1, 1:-1], padded[:, :-2, 1:-1, 1:-1],
            padded[:, 1:-1, 2:, 1:-1], padded[:, 1:-1, :-2, 1:-1],
            padded[:, 1:-1, 1:-1, 2:], padded[:, 1:-1, 1:-1, :-2]]


def prepare(viscous, spacing, pad_rule):
    neighbours = neighbours_of(pad_rule(viscous))
    faces = [(viscous + other) * 0.5 for other in neighbours]
    total = faces[0]
    for face in faces[1:]:
        total = total + face
    diagonal = total / (spacing * spacing)
    weight = jnp.concatenate([jnp.broadcast_to(OMEGA / diagonal, (3,) + diagonal.shape[1:]), BETA * viscous], axis=0)
    return faces, weight


def operate(field, faces, spacing, padded):
    neighbours = neighbours_of(padded)
    total = faces[0] * (field[:3] - neighbours[0][:3])
    for index in range(1, 6):
        total = total + faces[index] * (field[:3] - neighbours[index][:3])
    gradient = jnp.concatenate([neighbours[0][3:4] - neighbours[1][3:4],
                                neighbours[2][3:4] - neighbours[3][3:4],
                                neighbours[4][3:4] - neighbours[5][3:4]], axis=0)
    velocity = total / (spacing * spacing) + gradient / (2.0 * spacing)
    divergence = (neighbours[0][0:1] - neighbours[1][0:1]) + (neighbours[2][1:2] - neighbours[3][1:2]) + (neighbours[4][2:3] - neighbours[5][2:3])
    return jnp.concatenate([velocity, divergence / (2.0 * spacing)], axis=0)


def residual_of(source, field, faces, spacing, pad_rule):
    return source - operate(field, faces, spacing, pad_rule(field))


def smooth(source, field, faces, weight, spacing, pad_rule, count):
    for sweep in range(count):
        field = field + weight * residual_of(source, field, faces, spacing, pad_rule)
    return field


def restrict(array):
    comps, xsize, ysize, zsize = array.shape
    return array.reshape(comps, xsize // 2, 2, ysize // 2, 2, zsize // 2, 2).mean(axis=(2, 4, 6))


def prolong(array):
    return jnp.repeat(jnp.repeat(jnp.repeat(array, 2, axis=1), 2, axis=2), 2, axis=3)


def reference(forcing, viscosity):
    viscous = viscosity[None]
    faces_fine, weight_fine = prepare(viscous, 1.0, zero_pad)
    field = weight_fine * forcing
    field = smooth(forcing, field, faces_fine, weight_fine, 1.0, zero_pad, NU - 1)
    source_mid = restrict(residual_of(forcing, field, faces_fine, 1.0, zero_pad))
    viscous_mid = restrict(viscous)
    faces_mid, weight_mid = prepare(viscous_mid, 2.0, zero_pad)
    update_mid = weight_mid * source_mid
    update_mid = smooth(source_mid, update_mid, faces_mid, weight_mid, 2.0, zero_pad, NU - 1)
    source_low = restrict(residual_of(source_mid, update_mid, faces_mid, 2.0, zero_pad))
    viscous_low = restrict(viscous_mid)
    faces_low, weight_low = prepare(viscous_low, 4.0, zero_pad)
    update_low = weight_low * source_low
    update_low = smooth(source_low, update_low, faces_low, weight_low, 4.0, zero_pad, COARSE - 1)
    update_mid = update_mid + prolong(update_low)
    update_mid = smooth(source_mid, update_mid, faces_mid, weight_mid, 2.0, zero_pad, NU)
    field = field + prolong(update_mid)
    field = smooth(forcing, field, faces_fine, weight_fine, 1.0, zero_pad, NU)
    return field, residual_of(forcing, field, faces_fine, 1.0, zero_pad)
```

```python
import functools

import jax
import jax.numpy as jnp
from jax import lax
from jax.experimental import pallas as pl
from jax.experimental.pallas import tpu as pltpu
from jax.sharding import PartitionSpec as P

OMEGA = 0.6
BETA = 0.25
COARSE = 6
MESH = pl.DeviceIdType.MESH

H0, H1 = 3, 4
HF, HV = 2, 3
NEAR = 2


def over(lo, hi, block, body):
    count = hi - lo
    full = count // block
    if full > 1:

        def step(i, carry):
            body(lo + i * block, block)
            return carry

        lax.fori_loop(0, full, step, 0)
    elif full == 1:
        body(lo, block)
    if count % block:
        body(lo + full * block, count % block)


def kernel(G, D, yl, xl, Z, f_in, v_in, x_out, r_out,
           RF, RV, E0, B0, U0a, U0b, C0, E1, B1, U1a, U1b, C1, E2, B2, U2a, U2b, C2,
           EPs, EPr, EP2r, QBs, QBr, QYs, QYr, QZs, QZr,
           local_sem, s1, r1, s2, r2):
    X = G * xl
    n1, n2 = yl // 2, yl // 4
    H2 = NEAR * n2
    g = lax.axis_index("grp")
    d = lax.axis_index("dev")
    f32 = jnp.float32

    own_f = pltpu.make_async_copy(f_in, RF.at[g, :, pl.ds(HF, yl)], local_sem.at[0])
    own_v = pltpu.make_async_copy(v_in, RV.at[g, pl.ds(HV, yl)], local_sem.at[1])
    own_v.start()
    own_f.start()

    barrier = pltpu.get_barrier_semaphore()
    has = {k: jnp.logical_and(d + k >= 0, d + k < D) for k in (-2, -1, 1, 2)}
    expected = G - 1
    for j in range(1, G):
        pl.semaphore_signal(barrier, inc=1, device_id=(lax.rem(g + j, G), d), device_id_type=MESH)
    for k in (-1, 1):
        @pl.when(has[k])
        def _(k=k):
            for j in range(G):
                pl.semaphore_signal(
                    barrier, inc=1, device_id=(lax.rem(g + j, G), d + k), device_id_type=MESH)
        expected = expected + G * has[k].astype(jnp.int32)
    for k in (-2, 2):
        @pl.when(has[k])
        def _(k=k):
            pl.semaphore_signal(barrier, inc=1, device_id=(g, d + k), device_id_type=MESH)
        expected = expected + has[k].astype(jnp.int32)

    @pl.when(d == 0)
    def _():
        RV[:, 0:HV] = jnp.zeros((G, HV, xl, Z), f32)
        RF[:, :, 0:HF] = jnp.zeros((G, 4, HF, xl, Z), f32)
        U0b[:, 0:2] = jnp.zeros((4, 2, X, Z), f32)
        EPr[0] = jnp.zeros((2, X, Z), f32)
        QBr[0] = jnp.zeros((3, X, Z), f32)
        QYr[0] = jnp.zeros((4, X, Z), f32)
        QZr[1] = jnp.zeros((X, Z), f32)

    @pl.when(d < 2)
    def _():
        EP2r[0] = jnp.zeros((X, Z), f32)
        QZr[0] = jnp.zeros((X, Z), f32)

    @pl.when(d == D - 1)
    def _():
        RV[:, HV + yl:] = jnp.zeros((G, HV, xl, Z), f32)
        RF[:, :, HF + yl:] = jnp.zeros((G, 4, HF, xl, Z), f32)
        U0b[:, yl + 4:] = jnp.zeros((4, 2, X, Z), f32)
        EPr[1] = jnp.zeros((2, X, Z), f32)
        QBr[1] = jnp.zeros((3, X, Z), f32)
        QYr[1] = jnp.zeros((4, X, Z), f32)
        QZr[2] = jnp.zeros((X, Z), f32)

    @pl.when(d >= D - 2)
    def _():
        EP2r[1] = jnp.zeros((X, Z), f32)
        QZr[3] = jnp.zeros((X, Z), f32)

    pl.semaphore_wait(barrier, expected)

    def rdma(src, dst, ss, rs, target):
        return pltpu.make_async_remote_copy(
            src_ref=src, dst_ref=dst, send_sem=ss, recv_sem=rs,
            device_id=target, device_id_type=MESH)

    def first(j, slot, source):
        other = lax.rem(g + j, G)
        at = other if source else g
        k = (0, 0, 1, 1, -1, -1)[slot]
        if slot % 2 == 0:
            rows, put = {0: (0, HV), 1: (yl - HV, 0), -1: (0, HV + yl)}[k]
            count = yl if k == 0 else HV
            src, dst = v_in.at[pl.ds(rows, count)], RV.at[at, pl.ds(put, count)]
        else:
            rows, put = {0: (0, HF), 1: (yl - HF, 0), -1: (0, HF + yl)}[k]
            count = yl if k == 0 else HF
            src, dst = f_in.at[:, pl.ds(rows, count)], RF.at[at, :, pl.ds(put, count)]
        return rdma(src, dst, s1.at[j, slot], r1.at[at, slot], (other, d + k))

    for k, slots in ((1, (2, 3)), (-1, (4, 5))):
        @pl.when(has[k])
        def _(slots=slots):
            for slot in slots:
                for j in range(G):
                    first(j, slot, False).start()
    for slot in (0, 1):
        for j in range(1, G):
            first(j, slot, False).start()

    lo1, hi1 = H1, H1 + n1
    later = {
        "e_up": (EPs.at[1], EPr.at[0], 1),
        "e_down": (EPs.at[0], EPr.at[1], -1),
        "e_up2": (EPs.at[1, 0], EP2r.at[0], 2),
        "e_down2": (EPs.at[0, 0], EP2r.at[1], -2),
        "b_up": (QBs.at[1], QBr.at[0], 1),
        "b_down": (QBs.at[0], QBr.at[1], -1),
        "x_up": (U0b.at[:, pl.ds(yl, 2)], U0b.at[:, pl.ds(0, 2)], 1),
        "x_down": (U0b.at[:, pl.ds(4, 2)], U0b.at[:, pl.ds(yl + 4, 2)], -1),
        "y_up": (QYs.at[1], QYr.at[0], 1),
        "y_down": (QYs.at[0], QYr.at[1], -1),
        "z_up2": (QZs, QZr.at[0], 2),
        "z_up": (QZs, QZr.at[1], 1),
        "z_down": (QZs, QZr.at[2], -1),
        "z_down2": (QZs, QZr.at[3], -2),
    }
    index_of = {name: i for i, name in enumerate(later)}

    def copy_of(name):
        src, dst, k = later[name]
        i = index_of[name]
        return rdma(src, dst, s2.at[i], r2.at[i], (g, d + k)), k

    def start(*names):
        for name in names:
            copy, k = copy_of(name)
            pl.when(has[k])(copy.start)

    def receive(*names):
        for name in names:
            copy, k = copy_of(name)
            pl.when(has[-k])(copy.wait_recv)

    def sent(*names):
        for name in names:
            copy, k = copy_of(name)
            pl.when(has[k])(copy.wait_send)

    sub = lax.broadcasted_iota(jnp.int32, (X, Z), 0)
    lane = lax.broadcasted_iota(jnp.int32, (X, Z), 1)

    def roll(value, shift, dim):
        axis = value.ndim - 2 + dim
        return pltpu.roll(value, shift % value.shape[axis], axis)

    def partner(value, s):
        value = value + jnp.where((sub & s) == 0, roll(value, -s, 0), roll(value, s, 0))
        return value + jnp.where((lane & s) == 0, roll(value, -s, 1), roll(value, s, 1))

    def spread(value, ids, dim, s):
        odd = (ids & s) != 0
        return (jnp.where(odd, roll(value, s, dim), value),
                jnp.where(odd, value, roll(value, -s, dim)))

    def pack4(c):
        so, lo = (sub & 1) != 0, (lane & 1) != 0
        return jnp.where(lo, jnp.where(so, c[3], c[2]), jnp.where(so, c[1], c[0]))

    def unpack4(packed):
        left, right = spread(packed, lane, 1, 1)
        return [*spread(left, sub, 0, 1), *spread(right, sub, 0, 1)]

    def pick4(c, ids):
        a, b = (ids & 1) != 0, (ids & 2) != 0
        return jnp.where(b, jnp.where(a, c[3], c[2]), jnp.where(a, c[1], c[0]))

    def spread4(packed, ids, dim):
        even, odd = spread(packed, ids, dim, 1)
        v0, v2 = spread(even, ids, dim, 2)
        v1, v3 = spread(odd, ids, dim, 2)
        return [v0, v1, v2, v3]

    def level(s, E, B, C, block):
        inside = ((sub < X - s), (sub >= s), (lane < Z - s), (lane >= s))
        half = [jnp.where(m, f32(0.5 / s), f32(0.0)) for m in inside]
        scale = 1.0 / (s * s)

        def coefficients(lo, hi):
            def body(r, n):
                e = E[pl.ds(r, n)]
                xs = [jnp.where(m, roll(e, sh, dim), 0.0)
                      for m, sh, dim in zip(inside, (-s, s, -s, s), (0, 0, 1, 1))]
                ys = [E[pl.ds(r + 1, n)], E[pl.ds(r - 1, n)]]
                fx = [(e + other) * (0.5 * scale) for other in xs]
                fy = [(e + other) * (0.5 * scale) for other in ys]
                diagonal = (fx[0] + fx[1]) + (fy[0] + fy[1]) + (fx[2] + fx[3])
                for i in range(4):
                    C[i, pl.ds(r, n)] = jnp.where(inside[i], fx[i], 0.0)
                C[4, pl.ds(r, n)] = fy[0]
                C[5, pl.ds(r, n)] = fy[1]
                real = e > 0.0
                C[6, pl.ds(r, n)] = jnp.where(real, OMEGA / jnp.where(real, diagonal, 1.0), 0.0)
                C[7, pl.ds(r, n)] = BETA * e
                C[8, pl.ds(r, n)] = diagonal
            over(lo, hi, block, body)

        def begin(U, lo, hi):
            def body(r, n):
                w = C[6, pl.ds(r, n)]
                for c in range(3):
                    U[c, pl.ds(r, n)] = w * B[c, pl.ds(r, n)]
                U[3, pl.ds(r, n)] = C[7, pl.ds(r, n)] * B[3, pl.ds(r, n)]
            over(lo, hi, block, body)

        def parts(U, r, n):
            coef = [C[i, pl.ds(r, n)] for i in range(6)]
            centre = [U[c, pl.ds(r, n)] for c in range(4)]
            rolled = []
            for c in range(4):
                u = centre[c]
                rolled.append([roll(u, -s, 0), roll(u, s, 0), roll(u, -s, 1), roll(u, s, 1),
                               U[c, pl.ds(r + 1, n)], U[c, pl.ds(r - 1, n)]])
            p = rolled[3]
            grad = [half[0] * p[0] - half[1] * p[1], (p[4] - p[5]) * (0.5 / s),
                    half[2] * p[2] - half[3] * p[3]]
            out = []
            for c in range(3):
                t = [coef[i] * rolled[c][i] for i in range(6)]
                total = (t[0] + t[1]) + (t[2] + t[3]) + (t[4] + t[5])
                out.append((B[c, pl.ds(r, n)] - grad[c]) + total)
            div = ((half[0] * rolled[0][0] - half[1] * rolled[0][1])
                   + (rolled[1][4] - rolled[1][5]) * (0.5 / s)
                   + (half[2] * rolled[2][2] - half[3] * rolled[2][3]))
            out.append(B[3, pl.ds(r, n)] - div)
            return centre, out

        def sweep(U, V, lo, hi, also=None):
            def body(r, n):
                centre, out = parts(U, r, n)
                w = C[6, pl.ds(r, n)]
                for c in range(3):
                    V[c, pl.ds(r, n)] = (1.0 - OMEGA) * centre[c] + w * out[c]
                V[3, pl.ds(r, n)] = centre[3] + C[7, pl.ds(r, n)] * out[3]
            over(lo, hi, block, body)

        def residual(U, r, n):
            centre, out = parts(U, r, n)
            diagonal = C[8, pl.ds(r, n)]
            return [out[c] - diagonal * centre[c] for c in range(3)] + [out[3]]

        return coefficients, begin, sweep, residual

    def restrict_rows(value, s):
        n = value.shape[0] // 2
        pairs = value.reshape(n, 2, X, Z)
        return partner(pairs[:, 0] + pairs[:, 1], s) * 0.125

    coef0, begin0, sweep0, res0 = level(1, E0, B0, C0, 2)
    coef1, begin1, sweep1, res1 = level(2, E1, B1, C1, 2)
    coef2, begin2, sweep2, res2 = level(4, E2, B2, C2, 2)

    def place_v(lo, hi):
        for i in range(G):
            E0[lo:hi, i * xl:(i + 1) * xl, :] = RV[i, lo:hi]

    def place_f(lo, hi):
        for i in range(G):
            for c in range(4):
                B0[c, lo + H0 - HF:hi + H0 - HF, i * xl:(i + 1) * xl, :] = RF[i, c, lo:hi]

    own_v.wait()
    for j in range(1, G):
        first(j, 0, True).wait_recv()
    place_v(HV, HV + yl)

    def coarse_e(r, n):
        E1[pl.ds(H1 + r, n)] = restrict_rows(E0[pl.ds(H0 + 2 * r, 2 * n)], 1)
    over(0, n1, 2, coarse_e)

    def coarse_e2(r, n):
        E2[pl.ds(H2 + r, n)] = restrict_rows(E1[pl.ds(H1 + 2 * r, 2 * n)], 2)
    over(0, n2, 2, coarse_e2)
    packed = pick4([E2[H2 + i] for i in range(n2)], sub)
    EPs[0, 0] = packed
    EPs[1, 0] = packed
    EPs[0, 1] = pack4([E1[lo1 + i] for i in range(4)])
    EPs[1, 1] = pack4([E1[hi1 - 4 + i] for i in range(4)])
    start("e_up", "e_down", "e_up2", "e_down2")

    own_f.wait()
    for j in range(1, G):
        first(j, 1, True).wait_recv()
    place_f(HF, HF + yl)
    top, end = H0, H0 + yl
    coef0(top + 1, end - 1)
    begin0(U0a, top + 1, end - 1)
    sweep0(U0a, U0b, top + 2, end - 2)

    for k, slots in ((1, (2, 3)), (-1, (4, 5))):
        @pl.when(has[-k])
        def _(slots=slots):
            for slot in slots:
                for j in range(G):
                    first(j, slot, True).wait_recv()
    for a, b in ((0, HV), (HV + yl, 2 * HV + yl)):
        place_v(a, b)
    for a, b in ((0, HF), (HF + yl, 2 * HF + yl)):
        place_f(a, b)
    for a, b in ((top - 2, top + 1), (end - 1, end + 2)):
        coef0(a, b)
        begin0(U0a, a, b)
    for a, b in ((top - 1, top + 2), (end - 2, end + 1)):
        sweep0(U0a, U0b, a, b)

    def coarse_b(r, n):
        for c, value in enumerate(res0(U0b, H0 + 2 * r, 2 * n)):
            B1[c, pl.ds(H1 + r, n)] = restrict_rows(value, 1)
    over(0, n1, 1, coarse_b)
    for i in range(3):
        QBs[0, i] = pack4([B1[c, lo1 + i] for c in range(4)])
        QBs[1, i] = pack4([B1[c, hi1 - 3 + i] for c in range(4)])
    start("b_up", "b_down", "x_up", "x_down")

    receive("e_up", "e_down", "e_up2", "e_down2")
    for i, value in enumerate(unpack4(EPr[0, 1])):
        E1[i] = value
    for i, value in enumerate(unpack4(EPr[1, 1])):
        E1[hi1 + i] = value
    for at, value in ((0, EP2r[0]), (n2, EPr[0, 0]), (H2 + n2, EPr[1, 0]), (H2 + 2 * n2, EP2r[1])):
        for i, row in enumerate(spread4(value, sub, 0)):
            E2[at + i] = row
    coef1(lo1 - 3, hi1 + 3)
    coef2(1, 2 * H2 + n2 - 1)
    begin1(U1a, lo1, hi1)
    receive("b_up", "b_down")
    for i in range(3):
        for c, value in enumerate(unpack4(QBr[0, i])):
            B1[c, lo1 - 3 + i] = value
        for c, value in enumerate(unpack4(QBr[1, i])):
            B1[c, hi1 + i] = value
    begin1(U1a, lo1 - 2, lo1)
    begin1(U1a, hi1, hi1 + 2)
    sweep1(U1a, U1b, lo1 - 1, hi1 + 1)

    def coarse_b2(r, n):
        for c, value in enumerate(res1(U1b, H1 + 2 * r, 2 * n)):
            B2[c, pl.ds(H2 + r, n)] = restrict_rows(value, 2)
    over(0, n2, 1, coarse_b2)
    QZs[...] = pick4([pick4([B2[c, H2 + i] for c in range(4)], lane) for i in range(n2)], sub)
    start("z_up2", "z_down2", "z_up", "z_down")
    for i in range(4):
        QYs[0, i] = pack4([U1b[c, lo1 + i] for c in range(4)])
        QYs[1, i] = pack4([U1b[c, hi1 - 4 + i] for c in range(4)])
    start("y_up", "y_down")

    lo2, hi2 = H2, H2 + n2
    receive("z_up2", "z_up", "z_down", "z_down2")
    for slot, at in enumerate((0, n2, H2 + n2, H2 + 2 * n2)):
        for c, field in enumerate(spread4(QZr[slot], lane, 1)):
            for i, row in enumerate(spread4(field, sub, 0)):
                B2[c, at + i] = row
    begin2(U2a, lo2 - COARSE - 1, hi2 + COARSE + 1)
    here, there = U2a, U2b
    for i in range(COARSE - 1):
        ext = COARSE - i
        sweep2(here, there, lo2 - ext, hi2 + ext)
        here, there = there, here

    receive("y_up", "y_down")
    for i in range(4):
        for c, value in enumerate(unpack4(QYr[0, i])):
            U1b[c, lo1 - 4 + i] = value
        for c, value in enumerate(unpack4(QYr[1, i])):
            U1b[c, hi1 + i] = value

    def add1(r, n):
        for c in range(4):
            z = here[c, lo2 - 2 + r]
            U1b[c, pl.ds(2 * r, 2)] = U1b[c, pl.ds(2 * r, 2)] + z[None]
    over(0, n2 + 4, 1, add1)
    sweep1(U1b, U1a, lo1 - 3, hi1 + 3)
    sweep1(U1a, U1b, lo1 - 2, hi1 + 2)

    receive("x_up", "x_down")
    sent("x_up", "x_down")

    def add0(r, n):
        for c in range(4):
            y = U1b[c, lo1 - 1 + r]
            U0b[c, pl.ds(H0 - 2 + 2 * r, 2)] = U0b[c, pl.ds(H0 - 2 + 2 * r, 2)] + y[None]
    over(0, n1 + 2, 1, add0)
    for c in range(4):
        U0b[c, 0] = U0b[c, 0] + U1b[c, lo1 - 2]
        U0b[c, yl + 5] = U0b[c, yl + 5] + U1b[c, hi1 + 1]
    sweep0(U0b, U0a, top - 2, end + 2)
    sweep0(U0a, U0b, top - 1, end + 1)

    def finish(r, n):
        for c, value in enumerate(res0(U0b, H0 + r, n)):
            r_out[c, pl.ds(r, n)] = value
            x_out[c, pl.ds(r, n)] = U0b[c, pl.ds(H0 + r, n)]
    over(0, yl, 2, finish)

    for k, slots in ((1, (2, 3)), (-1, (4, 5))):
        @pl.when(has[k])
        def _(slots=slots):
            for slot in slots:
                for j in range(G):
                    first(j, slot, False).wait_send()
    for slot in (0, 1):
        for j in range(1, G):
            first(j, slot, False).wait_send()
    sent(*[name for name in later if not name.startswith("x_")])


def local(G, D, forcing, viscosity):
    _, xl, yl, Z = forcing.shape
    X = G * xl
    assert yl == 16 and xl % 4 == 0 and D > NEAR
    n1, n2 = yl // 2, yl // 4
    rows0, rows1, rows2 = yl + 2 * H0, n1 + 2 * H1, n2 * (1 + 2 * NEAR)
    f32 = jnp.float32
    vm = lambda *shape: pltpu.VMEM(shape, f32)
    sem = pltpu.SemaphoreType.DMA
    out = jax.ShapeDtypeStruct((4, yl, X, Z), f32)
    field = lambda rows: vm(4, rows, X, Z)
    any_spec = pl.BlockSpec(memory_space=pl.ANY)
    vmem_spec = pl.BlockSpec(memory_space=pltpu.VMEM)
    solved, left = pl.pallas_call(
        functools.partial(kernel, G, D, yl, xl, Z),
        out_shape=(out, out),
        in_specs=[any_spec, any_spec],
        out_specs=(vmem_spec, vmem_spec),
        scratch_shapes=[
            vm(G, 4, yl + 2 * HF, xl, Z), vm(G, yl + 2 * HV, xl, Z),
            vm(rows0, X, Z), field(rows0), field(rows0), field(rows0), vm(9, rows0, X, Z),
            vm(rows1, X, Z), field(rows1), field(rows1), field(rows1), vm(9, rows1, X, Z),
            vm(rows2, X, Z), field(rows2), field(rows2), field(rows2), vm(9, rows2, X, Z),
            vm(2, 2, X, Z), vm(2, 2, X, Z), vm(2, X, Z),
            vm(2, 3, X, Z), vm(2, 3, X, Z),
            vm(2, 4, X, Z), vm(2, 4, X, Z),
            vm(X, Z), vm(4, X, Z),
            sem((2,)), sem((G, 6)), sem((G, 6)), sem((14,)), sem((14,)),
        ],
        compiler_params=pltpu.CompilerParams(
            collective_id=0, has_side_effects=True, vmem_limit_bytes=50 * 1024 * 1024),
    )(jnp.transpose(forcing, (0, 2, 1, 3)), jnp.transpose(viscosity, (1, 0, 2)))
    at = lax.axis_index("grp") * xl

    def mine(array):
        part = lax.dynamic_slice_in_dim(array, at, xl, 2)
        return jnp.transpose(part, (0, 2, 1, 3))

    return mine(solved), mine(left)


def solution(mesh):
    G, D = mesh.shape["grp"], mesh.shape["dev"]
    in_specs = (P(None, "grp", "dev", None), P("grp", "dev", None))
    out_specs = (P(None, "grp", "dev", None), P(None, "grp", "dev", None))
    return jax.shard_map(
        functools.partial(local, G, D), mesh=mesh, in_specs=in_specs, out_specs=out_specs,
        check_vma=False)
```

```python
import functools

import jax
import jax.numpy as jnp
from jax import lax
from jax.experimental import pallas as pl
from jax.experimental.pallas import tpu as pltpu
from jax.sharding import PartitionSpec as P

OMEGA = 0.6
BETA = 0.25
COARSE = 6
MESH = pl.DeviceIdType.MESH

H0, H1 = 3, 4
HF, HV = 2, 3
NEAR = 2


def over(lo, hi, body, most=10):
    count = hi - lo
    steps = -(-count // most)
    while count % steps:
        steps += 1
    block = count // steps

    def step(i, carry):
        for j in range(block):
            body(lo + i * block + j, 1)
        return carry

    if steps == 1:
        step(0, 0)
    else:
        lax.fori_loop(0, steps, step, 0)


def kernel(G, D, yl, xl, Z, f_in, v_in, x_out, r_out,
           RF, RV, E0, B0, U0a, U0b, C0, E1, B1, U1a, U1b, C1, E2, B2, U2a, U2b, C2,
           EPs, EPr, EP2r, QBs, QBr, QYs, QYr, QZs, QZr,
           local_sem, s1, r1, s2, r2):
    X = G * xl
    n1, n2 = yl // 2, yl // 4
    H2 = NEAR * n2
    g = lax.axis_index("grp")
    d = lax.axis_index("dev")
    f32 = jnp.float32

    own_f = pltpu.make_async_copy(f_in, RF.at[g, :, pl.ds(HF, yl)], local_sem.at[0])
    own_v = pltpu.make_async_copy(v_in, RV.at[g, pl.ds(HV, yl)], local_sem.at[1])
    own_v.start()
    own_f.start()

    barrier = pltpu.get_barrier_semaphore()
    has = {k: jnp.logical_and(d + k >= 0, d + k < D) for k in (-2, -1, 1, 2)}
    expected = G - 1
    for j in range(1, G):
        pl.semaphore_signal(barrier, inc=1, device_id=(lax.rem(g + j, G), d), device_id_type=MESH)
    for k in (-1, 1):
        @pl.when(has[k])
        def _(k=k):
            for j in range(G):
                pl.semaphore_signal(
                    barrier, inc=1, device_id=(lax.rem(g + j, G), d + k), device_id_type=MESH)
        expected = expected + G * has[k].astype(jnp.int32)
    for k in (-2, 2):
        @pl.when(has[k])
        def _(k=k):
            pl.semaphore_signal(barrier, inc=1, device_id=(g, d + k), device_id_type=MESH)
        expected = expected + has[k].astype(jnp.int32)

    @pl.when(d == 0)
    def _():
        RV[:, 0:HV] = jnp.zeros((G, HV, xl, Z), f32)
        RF[:, :, 0:HF] = jnp.zeros((G, 4, HF, xl, Z), f32)
        U0b[:, 0:2] = jnp.zeros((4, 2, X, Z), f32)
        EPr[0] = jnp.zeros((2, X, Z), f32)
        QBr[0] = jnp.zeros((3, X, Z), f32)
        QYr[0] = jnp.zeros((4, X, Z), f32)
        QZr[1] = jnp.zeros((X, Z), f32)

    @pl.when(d < 2)
    def _():
        EP2r[0] = jnp.zeros((X, Z), f32)
        QZr[0] = jnp.zeros((X, Z), f32)

    @pl.when(d == D - 1)
    def _():
        RV[:, HV + yl:] = jnp.zeros((G, HV, xl, Z), f32)
        RF[:, :, HF + yl:] = jnp.zeros((G, 4, HF, xl, Z), f32)
        U0b[:, yl + 4:] = jnp.zeros((4, 2, X, Z), f32)
        EPr[1] = jnp.zeros((2, X, Z), f32)
        QBr[1] = jnp.zeros((3, X, Z), f32)
        QYr[1] = jnp.zeros((4, X, Z), f32)
        QZr[2] = jnp.zeros((X, Z), f32)

    @pl.when(d >= D - 2)
    def _():
        EP2r[1] = jnp.zeros((X, Z), f32)
        QZr[3] = jnp.zeros((X, Z), f32)

    pl.semaphore_wait(barrier, expected)

    def rdma(src, dst, ss, rs, target):
        return pltpu.make_async_remote_copy(
            src_ref=src, dst_ref=dst, send_sem=ss, recv_sem=rs,
            device_id=target, device_id_type=MESH)

    def first(j, slot, source):
        other = lax.rem(g + j, G)
        at = other if source else g
        k = (0, 0, 1, 1, -1, -1)[slot]
        if slot % 2 == 0:
            rows, put = {0: (0, HV), 1: (yl - HV, 0), -1: (0, HV + yl)}[k]
            count = yl if k == 0 else HV
            src, dst = v_in.at[pl.ds(rows, count)], RV.at[at, pl.ds(put, count)]
        else:
            rows, put = {0: (0, HF), 1: (yl - HF, 0), -1: (0, HF + yl)}[k]
            count = yl if k == 0 else HF
            src, dst = f_in.at[:, pl.ds(rows, count)], RF.at[at, :, pl.ds(put, count)]
        return rdma(src, dst, s1.at[j, slot], r1.at[at, slot], (other, d + k))

    for k, slots in ((1, (2, 3)), (-1, (4, 5))):
        @pl.when(has[k])
        def _(slots=slots):
            for slot in slots:
                for j in range(G):
                    first(j, slot, False).start()
    for slot in (0, 1):
        for j in range(1, G):
            first(j, slot, False).start()

    lo1, hi1 = H1, H1 + n1
    later = {
        "e_up": (EPs.at[1], EPr.at[0], 1),
        "e_down": (EPs.at[0], EPr.at[1], -1),
        "e_up2": (EPs.at[1, 0], EP2r.at[0], 2),
        "e_down2": (EPs.at[0, 0], EP2r.at[1], -2),
        "b_up": (QBs.at[1], QBr.at[0], 1),
        "b_down": (QBs.at[0], QBr.at[1], -1),
        "x_up": (U0b.at[:, pl.ds(yl, 2)], U0b.at[:, pl.ds(0, 2)], 1),
        "x_down": (U0b.at[:, pl.ds(4, 2)], U0b.at[:, pl.ds(yl + 4, 2)], -1),
        "y_up": (QYs.at[1], QYr.at[0], 1),
        "y_down": (QYs.at[0], QYr.at[1], -1),
        "z_up2": (QZs, QZr.at[0], 2),
        "z_up": (QZs, QZr.at[1], 1),
        "z_down": (QZs, QZr.at[2], -1),
        "z_down2": (QZs, QZr.at[3], -2),
    }
    index_of = {name: i for i, name in enumerate(later)}

    def copy_of(name):
        src, dst, k = later[name]
        i = index_of[name]
        return rdma(src, dst, s2.at[i], r2.at[i], (g, d + k)), k

    def start(*names):
        for name in names:
            copy, k = copy_of(name)
            pl.when(has[k])(copy.start)

    def receive(*names):
        for name in names:
            copy, k = copy_of(name)
            pl.when(has[-k])(copy.wait_recv)

    def sent(*names):
        for name in names:
            copy, k = copy_of(name)
            pl.when(has[k])(copy.wait_send)

    sub = lax.broadcasted_iota(jnp.int32, (X, Z), 0)
    lane = lax.broadcasted_iota(jnp.int32, (X, Z), 1)

    def roll(value, shift, dim):
        axis = value.ndim - 2 + dim
        return pltpu.roll(value, shift % value.shape[axis], axis)

    def partner(value, s):
        value = value + jnp.where((sub & s) == 0, roll(value, -s, 0), roll(value, s, 0))
        return value + jnp.where((lane & s) == 0, roll(value, -s, 1), roll(value, s, 1))

    def spread(value, ids, dim, s):
        odd = (ids & s) != 0
        return (jnp.where(odd, roll(value, s, dim), value),
                jnp.where(odd, value, roll(value, -s, dim)))

    def pack4(c):
        so, lo = (sub & 1) != 0, (lane & 1) != 0
        return jnp.where(lo, jnp.where(so, c[3], c[2]), jnp.where(so, c[1], c[0]))

    def unpack4(packed):
        left, right = spread(packed, lane, 1, 1)
        return [*spread(left, sub, 0, 1), *spread(right, sub, 0, 1)]

    def pick4(c, ids):
        a, b = (ids & 1) != 0, (ids & 2) != 0
        return jnp.where(b, jnp.where(a, c[3], c[2]), jnp.where(a, c[1], c[0]))

    def spread4(packed, ids, dim):
        even, odd = spread(packed, ids, dim, 1)
        v0, v2 = spread(even, ids, dim, 2)
        v1, v3 = spread(odd, ids, dim, 2)
        return [v0, v1, v2, v3]

    def level(s, E, B, C):
        inside = ((sub < X - s), (sub >= s), (lane < Z - s), (lane >= s))
        half = [jnp.where(m, f32(0.5 / s), f32(0.0)) for m in inside]
        scale = 1.0 / (s * s)

        def coefficients(lo, hi):
            def body(r, n):
                e = E[pl.ds(r, n)]
                xs = [jnp.where(m, roll(e, sh, dim), 0.0)
                      for m, sh, dim in zip(inside, (-s, s, -s, s), (0, 0, 1, 1))]
                ys = [E[pl.ds(r + 1, n)], E[pl.ds(r - 1, n)]]
                fx = [(e + other) * (0.5 * scale) for other in xs]
                fy = [(e + other) * (0.5 * scale) for other in ys]
                diagonal = (fx[0] + fx[1]) + (fy[0] + fy[1]) + (fx[2] + fx[3])
                for i in range(4):
                    C[i, pl.ds(r, n)] = jnp.where(inside[i], fx[i], 0.0)
                C[4, pl.ds(r, n)] = fy[0]
                C[5, pl.ds(r, n)] = fy[1]
                real = e > 0.0
                C[6, pl.ds(r, n)] = jnp.where(real, OMEGA / jnp.where(real, diagonal, 1.0), 0.0)
                C[7, pl.ds(r, n)] = BETA * e
                C[8, pl.ds(r, n)] = diagonal
            over(lo, hi, body)

        def begin(U, lo, hi):
            def body(r, n):
                w = C[6, pl.ds(r, n)]
                for c in range(3):
                    U[c, pl.ds(r, n)] = w * B[c, pl.ds(r, n)]
                U[3, pl.ds(r, n)] = C[7, pl.ds(r, n)] * B[3, pl.ds(r, n)]
            over(lo, hi, body)

        def parts(U, r, n):
            coef = [C[i, pl.ds(r, n)] for i in range(6)]
            centre = [U[c, pl.ds(r, n)] for c in range(4)]
            rolled = []
            for c in range(4):
                u = centre[c]
                rolled.append([roll(u, -s, 0), roll(u, s, 0), roll(u, -s, 1), roll(u, s, 1),
                               U[c, pl.ds(r + 1, n)], U[c, pl.ds(r - 1, n)]])
            p = rolled[3]
            grad = [half[0] * p[0] - half[1] * p[1], (p[4] - p[5]) * (0.5 / s),
                    half[2] * p[2] - half[3] * p[3]]
            out = []
            for c in range(3):
                t = [coef[i] * rolled[c][i] for i in range(6)]
                total = (t[0] + t[1]) + (t[2] + t[3]) + (t[4] + t[5])
                out.append((B[c, pl.ds(r, n)] - grad[c]) + total)
            div = ((half[0] * rolled[0][0] - half[1] * rolled[0][1])
                   + (rolled[1][4] - rolled[1][5]) * (0.5 / s)
                   + (half[2] * rolled[2][2] - half[3] * rolled[2][3]))
            out.append(B[3, pl.ds(r, n)] - div)
            return centre, out

        def sweep(U, V, lo, hi, also=None):
            def body(r, n):
                centre, out = parts(U, r, n)
                w = C[6, pl.ds(r, n)]
                for c in range(3):
                    V[c, pl.ds(r, n)] = (1.0 - OMEGA) * centre[c] + w * out[c]
                V[3, pl.ds(r, n)] = centre[3] + C[7, pl.ds(r, n)] * out[3]
            over(lo, hi, body)

        def residual(U, r, n):
            centre, out = parts(U, r, n)
            diagonal = C[8, pl.ds(r, n)]
            return [out[c] - diagonal * centre[c] for c in range(3)] + [out[3]]

        return coefficients, begin, sweep, residual

    def restrict_rows(value, s):
        n = value.shape[0] // 2
        pairs = value.reshape(n, 2, X, Z)
        return partner(pairs[:, 0] + pairs[:, 1], s) * 0.125

    coef0, begin0, sweep0, res0 = level(1, E0, B0, C0)
    coef1, begin1, sweep1, res1 = level(2, E1, B1, C1)
    coef2, begin2, sweep2, res2 = level(4, E2, B2, C2)

    def place_v(lo, hi):
        for i in range(G):
            E0[lo:hi, i * xl:(i + 1) * xl, :] = RV[i, lo:hi]

    def place_f(lo, hi):
        for i in range(G):
            for c in range(4):
                B0[c, lo + H0 - HF:hi + H0 - HF, i * xl:(i + 1) * xl, :] = RF[i, c, lo:hi]

    own_v.wait()
    for j in range(1, G):
        first(j, 0, True).wait_recv()
    place_v(HV, HV + yl)

    def coarse_e(r, n):
        E1[pl.ds(H1 + r, n)] = restrict_rows(E0[pl.ds(H0 + 2 * r, 2 * n)], 1)
    over(0, n1, coarse_e)

    def coarse_e2(r, n):
        E2[pl.ds(H2 + r, n)] = restrict_rows(E1[pl.ds(H1 + 2 * r, 2 * n)], 2)
    over(0, n2, coarse_e2)
    packed = pick4([E2[H2 + i] for i in range(n2)], sub)
    EPs[0, 0] = packed
    EPs[1, 0] = packed
    EPs[0, 1] = pack4([E1[lo1 + i] for i in range(4)])
    EPs[1, 1] = pack4([E1[hi1 - 4 + i] for i in range(4)])
    start("e_up", "e_down", "e_up2", "e_down2")

    own_f.wait()
    for j in range(1, G):
        first(j, 1, True).wait_recv()
    place_f(HF, HF + yl)
    top, end = H0, H0 + yl
    coef0(top + 1, end - 1)
    begin0(U0a, top + 1, end - 1)
    sweep0(U0a, U0b, top + 2, end - 2)

    for k, slots in ((1, (2, 3)), (-1, (4, 5))):
        @pl.when(has[-k])
        def _(slots=slots):
            for slot in slots:
                for j in range(G):
                    first(j, slot, True).wait_recv()
    for a, b in ((0, HV), (HV + yl, 2 * HV + yl)):
        place_v(a, b)
    for a, b in ((0, HF), (HF + yl, 2 * HF + yl)):
        place_f(a, b)
    for a, b in ((top - 2, top + 1), (end - 1, end + 2)):
        coef0(a, b)
        begin0(U0a, a, b)
    for a, b in ((top - 1, top + 2), (end - 2, end + 1)):
        sweep0(U0a, U0b, a, b)

    def coarse_b(r, n):
        for c, value in enumerate(res0(U0b, H0 + 2 * r, 2 * n)):
            B1[c, pl.ds(H1 + r, n)] = restrict_rows(value, 1)
    over(0, n1, coarse_b)
    for i in range(3):
        QBs[0, i] = pack4([B1[c, lo1 + i] for c in range(4)])
        QBs[1, i] = pack4([B1[c, hi1 - 3 + i] for c in range(4)])
    start("b_up", "b_down", "x_up", "x_down")

    receive("e_up", "e_down", "e_up2", "e_down2")
    for i, value in enumerate(unpack4(EPr[0, 1])):
        E1[i] = value
    for i, value in enumerate(unpack4(EPr[1, 1])):
        E1[hi1 + i] = value
    for at, value in ((0, EP2r[0]), (n2, EPr[0, 0]), (H2 + n2, EPr[1, 0]), (H2 + 2 * n2, EP2r[1])):
        for i, row in enumerate(spread4(value, sub, 0)):
            E2[at + i] = row
    coef1(lo1 - 3, hi1 + 3)
    coef2(1, 2 * H2 + n2 - 1)
    begin1(U1a, lo1, hi1)
    receive("b_up", "b_down")
    for i in range(3):
        for c, value in enumerate(unpack4(QBr[0, i])):
            B1[c, lo1 - 3 + i] = value
        for c, value in enumerate(unpack4(QBr[1, i])):
            B1[c, hi1 + i] = value
    begin1(U1a, lo1 - 2, lo1)
    begin1(U1a, hi1, hi1 + 2)
    sweep1(U1a, U1b, lo1 - 1, hi1 + 1)

    def coarse_b2(r, n):
        for c, value in enumerate(res1(U1b, H1 + 2 * r, 2 * n)):
            B2[c, pl.ds(H2 + r, n)] = restrict_rows(value, 2)
    over(0, n2, coarse_b2)
    QZs[...] = pick4([pick4([B2[c, H2 + i] for c in range(4)], lane) for i in range(n2)], sub)
    start("z_up2", "z_down2", "z_up", "z_down")
    for i in range(4):
        QYs[0, i] = pack4([U1b[c, lo1 + i] for c in range(4)])
        QYs[1, i] = pack4([U1b[c, hi1 - 4 + i] for c in range(4)])
    start("y_up", "y_down")

    lo2, hi2 = H2, H2 + n2
    receive("z_up2", "z_up", "z_down", "z_down2")
    for slot, at in enumerate((0, n2, H2 + n2, H2 + 2 * n2)):
        for c, field in enumerate(spread4(QZr[slot], lane, 1)):
            for i, row in enumerate(spread4(field, sub, 0)):
                B2[c, at + i] = row
    begin2(U2a, lo2 - COARSE - 1, hi2 + COARSE + 1)
    here, there = U2a, U2b
    for i in range(COARSE - 1):
        ext = COARSE - i
        sweep2(here, there, lo2 - ext, hi2 + ext)
        here, there = there, here

    receive("y_up", "y_down")
    for i in range(4):
        for c, value in enumerate(unpack4(QYr[0, i])):
            U1b[c, lo1 - 4 + i] = value
        for c, value in enumerate(unpack4(QYr[1, i])):
            U1b[c, hi1 + i] = value

    def add1(r, n):
        for c in range(4):
            z = here[c, lo2 - 2 + r]
            U1b[c, pl.ds(2 * r, 2)] = U1b[c, pl.ds(2 * r, 2)] + z[None]
    over(0, n2 + 4, add1)
    sweep1(U1b, U1a, lo1 - 3, hi1 + 3)
    sweep1(U1a, U1b, lo1 - 2, hi1 + 2)

    receive("x_up", "x_down")
    sent("x_up", "x_down")

    def add0(r, n):
        for c in range(4):
            y = U1b[c, lo1 - 1 + r]
            U0b[c, pl.ds(H0 - 2 + 2 * r, 2)] = U0b[c, pl.ds(H0 - 2 + 2 * r, 2)] + y[None]
    over(0, n1 + 2, add0)
    for c in range(4):
        U0b[c, 0] = U0b[c, 0] + U1b[c, lo1 - 2]
        U0b[c, yl + 5] = U0b[c, yl + 5] + U1b[c, hi1 + 1]
    sweep0(U0b, U0a, top - 2, end + 2)
    sweep0(U0a, U0b, top - 1, end + 1)

    def finish(r, n):
        for c, value in enumerate(res0(U0b, H0 + r, n)):
            r_out[c, pl.ds(r, n)] = value
            x_out[c, pl.ds(r, n)] = U0b[c, pl.ds(H0 + r, n)]
    over(0, yl, finish)

    for k, slots in ((1, (2, 3)), (-1, (4, 5))):
        @pl.when(has[k])
        def _(slots=slots):
            for slot in slots:
                for j in range(G):
                    first(j, slot, False).wait_send()
    for slot in (0, 1):
        for j in range(1, G):
            first(j, slot, False).wait_send()
    sent(*[name for name in later if not name.startswith("x_")])


def local(G, D, forcing, viscosity):
    _, xl, yl, Z = forcing.shape
    X = G * xl
    assert yl == 16 and xl % 4 == 0 and D > NEAR
    n1, n2 = yl // 2, yl // 4
    rows0, rows1, rows2 = yl + 2 * H0, n1 + 2 * H1, n2 * (1 + 2 * NEAR)
    f32 = jnp.float32
    vm = lambda *shape: pltpu.VMEM(shape, f32)
    sem = pltpu.SemaphoreType.DMA
    out = jax.ShapeDtypeStruct((4, yl, X, Z), f32)
    field = lambda rows: vm(4, rows, X, Z)
    any_spec = pl.BlockSpec(memory_space=pl.ANY)
    vmem_spec = pl.BlockSpec(memory_space=pltpu.VMEM)
    solved, left = pl.pallas_call(
        functools.partial(kernel, G, D, yl, xl, Z),
        out_shape=(out, out),
        in_specs=[any_spec, any_spec],
        out_specs=(vmem_spec, vmem_spec),
        scratch_shapes=[
            vm(G, 4, yl + 2 * HF, xl, Z), vm(G, yl + 2 * HV, xl, Z),
            vm(rows0, X, Z), field(rows0), field(rows0), field(rows0), vm(9, rows0, X, Z),
            vm(rows1, X, Z), field(rows1), field(rows1), field(rows1), vm(9, rows1, X, Z),
            vm(rows2, X, Z), field(rows2), field(rows2), field(rows2), vm(9, rows2, X, Z),
            vm(2, 2, X, Z), vm(2, 2, X, Z), vm(2, X, Z),
            vm(2, 3, X, Z), vm(2, 3, X, Z),
            vm(2, 4, X, Z), vm(2, 4, X, Z),
            vm(X, Z), vm(4, X, Z),
            sem((2,)), sem((G, 6)), sem((G, 6)), sem((14,)), sem((14,)),
        ],
        compiler_params=pltpu.CompilerParams(
            collective_id=0, has_side_effects=True, vmem_limit_bytes=50 * 1024 * 1024),
    )(jnp.transpose(forcing, (0, 2, 1, 3)), jnp.transpose(viscosity, (1, 0, 2)))
    at = lax.axis_index("grp") * xl

    def mine(array):
        part = lax.dynamic_slice_in_dim(array, at, xl, 2)
        return jnp.transpose(part, (0, 2, 1, 3))

    return mine(solved), mine(left)


def solution(mesh):
    G, D = mesh.shape["grp"], mesh.shape["dev"]
    in_specs = (P(None, "grp", "dev", None), P("grp", "dev", None))
    out_specs = (P(None, "grp", "dev", None), P(None, "grp", "dev", None))
    return jax.shard_map(
        functools.partial(local, G, D), mesh=mesh, in_specs=in_specs, out_specs=out_specs,
        check_vma=False)
```

```python
import functools

import jax
import jax.numpy as jnp
from jax import lax
from jax.experimental import pallas as pl
from jax.experimental.pallas import tpu as pltpu
from jax.sharding import PartitionSpec as P

OMEGA = 0.6
BETA = 0.25
COARSE = 6
MESH = pl.DeviceIdType.MESH

H0, H1 = 3, 2
HF, HV = 2, 3
NEAR = 2


def over(lo, hi, body, most=10):
    count = hi - lo
    steps = -(-count // most)
    while count % steps:
        steps += 1
    block = count // steps

    def step(i, carry):
        for j in range(block):
            body(lo + i * block + j)
        return carry

    if steps == 1:
        step(0, 0)
    else:
        lax.fori_loop(0, steps, step, 0)


def kernel(G, D, yl, xl, Z, f_in, v_in, x_out, r_out,
           RF, RV, E0, B0, U0a, U0b, C0, E1, B1, U1a, U1b, C1, E2, B2, U2a, U2b, C2,
           EPs, EPr, EP2r, QBs, QBr, QYs, QYr, QZs, QZr,
           local_sem, s1, r1, s2, r2):
    X = G * xl
    n1 = yl // 4
    g = lax.axis_index("grp")
    d = lax.axis_index("dev")
    f32 = jnp.float32

    own_f = pltpu.make_async_copy(f_in, RF.at[g, :, pl.ds(HF, yl)], local_sem.at[0])
    own_v = pltpu.make_async_copy(v_in, RV.at[g, pl.ds(HV, yl)], local_sem.at[1])
    own_v.start()
    own_f.start()

    barrier = pltpu.get_barrier_semaphore()
    has = {k: jnp.logical_and(d + k >= 0, d + k < D) for k in (-2, -1, 1, 2)}
    expected = G - 1
    for j in range(1, G):
        pl.semaphore_signal(barrier, inc=1, device_id=(lax.rem(g + j, G), d), device_id_type=MESH)
    for k in (-1, 1):
        @pl.when(has[k])
        def _(k=k):
            for j in range(G):
                pl.semaphore_signal(
                    barrier, inc=1, device_id=(lax.rem(g + j, G), d + k), device_id_type=MESH)
        expected = expected + G * has[k].astype(jnp.int32)
    for k in (-2, 2):
        @pl.when(has[k])
        def _(k=k):
            pl.semaphore_signal(barrier, inc=1, device_id=(g, d + k), device_id_type=MESH)
        expected = expected + has[k].astype(jnp.int32)

    @pl.when(d == 0)
    def _():
        RV[:, 0:HV] = jnp.zeros((G, HV, xl, Z), f32)
        RF[:, :, 0:HF] = jnp.zeros((G, 4, HF, xl, Z), f32)
        U0b[:, 0:2] = jnp.zeros((4, 2, X, Z), f32)
        EPr[0] = jnp.zeros((2, X, Z), f32)
        QBr[0] = jnp.zeros((2, 2, X, Z), f32)
        QYr[0] = jnp.zeros((2, 2, X, Z), f32)
        QZr[1] = jnp.zeros((X, Z), f32)

    @pl.when(d < 2)
    def _():
        EP2r[0] = jnp.zeros((X, Z), f32)
        QZr[0] = jnp.zeros((X, Z), f32)

    @pl.when(d == D - 1)
    def _():
        RV[:, HV + yl:] = jnp.zeros((G, HV, xl, Z), f32)
        RF[:, :, HF + yl:] = jnp.zeros((G, 4, HF, xl, Z), f32)
        U0b[:, yl + 4:] = jnp.zeros((4, 2, X, Z), f32)
        EPr[1] = jnp.zeros((2, X, Z), f32)
        QBr[1] = jnp.zeros((2, 2, X, Z), f32)
        QYr[1] = jnp.zeros((2, 2, X, Z), f32)
        QZr[2] = jnp.zeros((X, Z), f32)

    @pl.when(d >= D - 2)
    def _():
        EP2r[1] = jnp.zeros((X, Z), f32)
        QZr[3] = jnp.zeros((X, Z), f32)

    pl.semaphore_wait(barrier, expected)

    def rdma(src, dst, ss, rs, target):
        return pltpu.make_async_remote_copy(
            src_ref=src, dst_ref=dst, send_sem=ss, recv_sem=rs,
            device_id=target, device_id_type=MESH)

    def first(j, slot, source):
        other = lax.rem(g + j, G)
        at = other if source else g
        k = (0, 0, 1, 1, -1, -1)[slot]
        if slot % 2 == 0:
            rows, put = {0: (0, HV), 1: (yl - HV, 0), -1: (0, HV + yl)}[k]
            count = yl if k == 0 else HV
            src, dst = v_in.at[pl.ds(rows, count)], RV.at[at, pl.ds(put, count)]
        else:
            rows, put = {0: (0, HF), 1: (yl - HF, 0), -1: (0, HF + yl)}[k]
            count = yl if k == 0 else HF
            src, dst = f_in.at[:, pl.ds(rows, count)], RF.at[at, :, pl.ds(put, count)]
        return rdma(src, dst, s1.at[j, slot], r1.at[at, slot], (other, d + k))

    for k, slots in ((1, (2, 3)), (-1, (4, 5))):
        @pl.when(has[k])
        def _(slots=slots):
            for slot in slots:
                for j in range(G):
                    first(j, slot, False).start()
    for slot in (0, 1):
        for j in range(1, G):
            first(j, slot, False).start()

    lo1, hi1 = H1, H1 + n1
    later = {
        "e_up": (EPs.at[1], EPr.at[0], 1),
        "e_down": (EPs.at[0], EPr.at[1], -1),
        "e_up2": (EPs.at[1, 0], EP2r.at[0], 2),
        "e_down2": (EPs.at[0, 0], EP2r.at[1], -2),
        "b_up": (QBs.at[1], QBr.at[0], 1),
        "b_down": (QBs.at[0], QBr.at[1], -1),
        "x_up": (U0b.at[:, pl.ds(yl, 2)], U0b.at[:, pl.ds(0, 2)], 1),
        "x_down": (U0b.at[:, pl.ds(4, 2)], U0b.at[:, pl.ds(yl + 4, 2)], -1),
        "y_up": (QYs.at[1], QYr.at[0], 1),
        "y_down": (QYs.at[0], QYr.at[1], -1),
        "z_up2": (QZs, QZr.at[0], 2),
        "z_up": (QZs, QZr.at[1], 1),
        "z_down": (QZs, QZr.at[2], -1),
        "z_down2": (QZs, QZr.at[3], -2),
    }
    index_of = {name: i for i, name in enumerate(later)}

    def copy_of(name):
        src, dst, k = later[name]
        i = index_of[name]
        return rdma(src, dst, s2.at[i], r2.at[i], (g, d + k)), k

    def start(*names):
        for name in names:
            copy, k = copy_of(name)
            pl.when(has[k])(copy.start)

    def receive(*names):
        for name in names:
            copy, k = copy_of(name)
            pl.when(has[-k])(copy.wait_recv)

    def sent(*names):
        for name in names:
            copy, k = copy_of(name)
            pl.when(has[k])(copy.wait_send)

    sub = lax.broadcasted_iota(jnp.int32, (X, Z), 0)
    lane = lax.broadcasted_iota(jnp.int32, (X, Z), 1)

    def roll(value, shift, dim):
        axis = value.ndim - 2 + dim
        return pltpu.roll(value, shift % value.shape[axis], axis)

    def partner(value, s):
        value = value + jnp.where((sub & s) == 0, roll(value, -s, 0), roll(value, s, 0))
        return value + jnp.where((lane & s) == 0, roll(value, -s, 1), roll(value, s, 1))

    def spread(value, ids, dim, s):
        odd = (ids & s) != 0
        return (jnp.where(odd, roll(value, s, dim), value),
                jnp.where(odd, value, roll(value, -s, dim)))

    def pack2(c):
        return jnp.where((lane & 1) != 0, c[1], c[0])

    def unpack2(packed):
        return spread(packed, lane, 1, 1)

    def pick4(c, ids):
        a, b = (ids & 1) != 0, (ids & 2) != 0
        return jnp.where(b, jnp.where(a, c[3], c[2]), jnp.where(a, c[1], c[0]))

    def spread4(packed, ids, dim):
        even, odd = spread(packed, ids, dim, 1)
        v0, v2 = spread(even, ids, dim, 2)
        v1, v3 = spread(odd, ids, dim, 2)
        return [v0, v1, v2, v3]

    def next_of(get, i, s, last):
        if s == 1:
            return get(i + 1)
        return jnp.where((sub & (s - 1)) == s - 1,
                         roll(get(min(i + 1, last)), s - 1, 0), roll(get(i), -1, 0))

    def prev_of(get, i, s, last):
        if s == 1:
            return get(i - 1)
        return jnp.where((sub & (s - 1)) == 0,
                         roll(get(max(i - 1, 0)), 1 - s, 0), roll(get(i), 1, 0))

    def level(s, E, B, C):
        last = E.shape[0] - 1
        inside = ((sub < X - s), (sub >= s), (lane < Z - s), (lane >= s))
        half = [jnp.where(m, f32(0.5 / s), f32(0.0)) for m in inside]
        scale = 1.0 / (s * s)

        def coefficients(lo, hi):
            def body(r):
                e = E[r]
                xs = [jnp.where(m, roll(e, sh, dim), 0.0)
                      for m, sh, dim in zip(inside, (-s, s, -s, s), (0, 0, 1, 1))]
                get = lambda i: E[i]
                ys = [next_of(get, r, s, last), prev_of(get, r, s, last)]
                fx = [(e + other) * (0.5 * scale) for other in xs]
                fy = [(e + other) * (0.5 * scale) for other in ys]
                diagonal = (fx[0] + fx[1]) + (fy[0] + fy[1]) + (fx[2] + fx[3])
                for i in range(4):
                    C[i, r] = jnp.where(inside[i], fx[i], 0.0)
                C[4, r] = fy[0]
                C[5, r] = fy[1]
                real = e > 0.0
                C[6, r] = jnp.where(real, OMEGA / jnp.where(real, diagonal, 1.0), 0.0)
                C[7, r] = BETA * e
                C[8, r] = diagonal
            over(lo, hi, body)

        def begin(U, lo, hi):
            def body(r):
                w = C[6, r]
                for c in range(3):
                    U[c, r] = w * B[c, r]
                U[3, r] = C[7, r] * B[3, r]
            over(lo, hi, body)

        def parts(U, r):
            coef = [C[i, r] for i in range(6)]
            centre = [U[c, r] for c in range(4)]
            rolled = []
            for c in range(4):
                u = centre[c]
                rolled.append([roll(u, -s, 0), roll(u, s, 0), roll(u, -s, 1), roll(u, s, 1),
                               next_of(lambda i: U[c, i], r, s, last),
                               prev_of(lambda i: U[c, i], r, s, last)])
            p = rolled[3]
            grad = [half[0] * p[0] - half[1] * p[1], (p[4] - p[5]) * (0.5 / s),
                    half[2] * p[2] - half[3] * p[3]]
            out = []
            for c in range(3):
                t = [coef[i] * rolled[c][i] for i in range(6)]
                total = (t[0] + t[1]) + (t[2] + t[3]) + (t[4] + t[5])
                out.append((B[c, r] - grad[c]) + total)
            div = ((half[0] * rolled[0][0] - half[1] * rolled[0][1])
                   + (rolled[1][4] - rolled[1][5]) * (0.5 / s)
                   + (half[2] * rolled[2][2] - half[3] * rolled[2][3]))
            out.append(B[3, r] - div)
            return centre, out

        def sweep(U, V, lo, hi, also=None):
            def body(r):
                centre, out = parts(U, r)
                w = C[6, r]
                for c in range(3):
                    V[c, r] = (1.0 - OMEGA) * centre[c] + w * out[c]
                V[3, r] = centre[3] + C[7, r] * out[3]
            over(lo, hi, body)

        def residual(U, r):
            centre, out = parts(U, r)
            diagonal = C[8, r]
            return [out[c] - diagonal * centre[c] for c in range(3)] + [out[3]]

        return coefficients, begin, sweep, residual

    def restrict0(rows):
        return jnp.where((sub & 1) == 0, partner(rows[0] + rows[1], 1),
                         partner(rows[2] + rows[3], 1)) * 0.125

    def restrict1(tile):
        tile = tile + jnp.where((sub & 1) == 0, roll(tile, -1, 0), roll(tile, 1, 0))
        return partner(tile, 2) * 0.125

    coef0, begin0, sweep0, res0 = level(1, E0, B0, C0)
    coef1, begin1, sweep1, res1 = level(2, E1, B1, C1)
    coef2, begin2, sweep2, res2 = level(4, E2, B2, C2)

    def place_v(lo, hi):
        for i in range(G):
            E0[lo:hi, i * xl:(i + 1) * xl, :] = RV[i, lo:hi]

    def place_f(lo, hi):
        for i in range(G):
            for c in range(4):
                B0[c, lo + H0 - HF:hi + H0 - HF, i * xl:(i + 1) * xl, :] = RF[i, c, lo:hi]

    own_v.wait()
    for j in range(1, G):
        first(j, 0, True).wait_recv()
    place_v(HV, HV + yl)

    def coarse_e(r):
        E1[lo1 + r] = restrict0([E0[H0 + 4 * r + i] for i in range(4)])
    over(0, n1, coarse_e)
    packed = pick4([restrict1(E1[lo1 + i]) for i in range(n1)], sub)
    E2[NEAR] = packed
    EPs[0, 0] = packed
    EPs[1, 0] = packed
    EPs[0, 1] = pack2([E1[lo1], E1[lo1 + 1]])
    EPs[1, 1] = pack2([E1[hi1 - 2], E1[hi1 - 1]])
    start("e_up", "e_down", "e_up2", "e_down2")

    own_f.wait()
    for j in range(1, G):
        first(j, 1, True).wait_recv()
    place_f(HF, HF + yl)
    top, end = H0, H0 + yl
    coef0(top + 1, end - 1)
    begin0(U0a, top + 1, end - 1)
    sweep0(U0a, U0b, top + 2, end - 2)

    for k, slots in ((1, (2, 3)), (-1, (4, 5))):
        @pl.when(has[-k])
        def _(slots=slots):
            for slot in slots:
                for j in range(G):
                    first(j, slot, True).wait_recv()
    for a, b in ((0, HV), (HV + yl, 2 * HV + yl)):
        place_v(a, b)
    for a, b in ((0, HF), (HF + yl, 2 * HF + yl)):
        place_f(a, b)
    for a, b in ((top - 2, top + 1), (end - 1, end + 2)):
        coef0(a, b)
        begin0(U0a, a, b)
    for a, b in ((top - 1, top + 2), (end - 2, end + 1)):
        sweep0(U0a, U0b, a, b)

    def coarse_b(r):
        rows = [res0(U0b, H0 + 4 * r + i) for i in range(4)]
        for c in range(4):
            B1[c, lo1 + r] = restrict0([row[c] for row in rows])
    over(0, n1, coarse_b, 2)

    def pack_tiles(packed, U):
        for i in range(2):
            for half in range(2):
                pair = (2 * half, 2 * half + 1)
                packed[0, i, half] = pack2([U[c, lo1 + i] for c in pair])
                packed[1, i, half] = pack2([U[c, hi1 - 2 + i] for c in pair])

    def unpack_tiles(packed, U):
        for i in range(2):
            for half in range(2):
                for side, at in ((0, lo1 - 2), (1, hi1)):
                    for c, value in enumerate(unpack2(packed[side, i, half])):
                        U[2 * half + c, at + i] = value

    pack_tiles(QBs, B1)
    start("b_up", "b_down")

    receive("e_up", "e_down", "e_up2", "e_down2")
    for i in range(2):
        E1[i] = unpack2(EPr[0, 1])[i]
        E1[hi1 + i] = unpack2(EPr[1, 1])[i]
    for at, value in ((0, EP2r[0]), (1, EPr[0, 0]), (3, EPr[1, 0]), (4, EP2r[1])):
        E2[at] = value
    coef1(0, hi1 + 2)
    coef2(0, 2 * NEAR + 1)
    begin1(U1a, lo1, hi1)
    receive("b_up", "b_down")
    unpack_tiles(QBr, B1)
    begin1(U1a, lo1 - 2, lo1)
    begin1(U1a, hi1, hi1 + 2)
    sweep1(U1a, U1b, lo1 - 1, hi1 + 1)
    rows = []
    for i in range(n1):
        rows.append([restrict1(value) for value in res1(U1b, lo1 + i)])
    for c in range(4):
        B2[c, NEAR] = pick4([row[c] for row in rows], sub)
    QZs[...] = pick4([B2[c, NEAR] for c in range(4)], lane)
    start("z_up2", "z_down2", "z_up", "z_down")
    pack_tiles(QYs, U1b)
    start("y_up", "y_down", "x_up", "x_down")

    begin2(U2a, NEAR, NEAR + 1)
    receive("z_up2", "z_up", "z_down", "z_down2")
    for slot, at in enumerate((0, 1, 3, 4)):
        for c, field in enumerate(spread4(QZr[slot], lane, 1)):
            B2[c, at] = field
    begin2(U2a, 0, NEAR)
    begin2(U2a, NEAR + 1, 2 * NEAR + 1)
    here, there = U2a, U2b
    for i in range(COARSE - 1):
        sweep2(here, there, 0, 2 * NEAR + 1)
        here, there = there, here

    receive("y_up", "y_down")
    unpack_tiles(QYr, U1b)
    for c in range(4):
        below, own, above = [spread4(here[c, i], sub, 0) for i in (1, 2, 3)]
        for i, z in enumerate(below[2:] + own + above[:2]):
            U1b[c, i] = U1b[c, i] + z
    sweep1(U1b, U1a, 0, hi1 + 2)
    sweep1(U1a, U1b, lo1 - 1, hi1 + 1)

    receive("x_up", "x_down")
    sent("x_up", "x_down")

    def add0(r):
        for c in range(4):
            for i, y in enumerate(spread(U1b[c, lo1 + r], sub, 0, 1)):
                for at in (H0 + 4 * r + 2 * i, H0 + 4 * r + 2 * i + 1):
                    U0b[c, at] = U0b[c, at] + y
    over(0, n1, add0, 2)
    for c in range(4):
        low = spread(U1b[c, lo1 - 1], sub, 0, 1)
        high = spread(U1b[c, hi1], sub, 0, 1)
        for at, y in ((0, low[0]), (1, low[1]), (2, low[1]),
                      (yl + 3, high[0]), (yl + 4, high[0]), (yl + 5, high[1])):
            U0b[c, at] = U0b[c, at] + y
    sweep0(U0b, U0a, top - 2, end + 2)
    sweep0(U0a, U0b, top - 1, end + 1)

    def finish(r):
        for c, value in enumerate(res0(U0b, H0 + r)):
            r_out[c, r] = value
            x_out[c, r] = U0b[c, H0 + r]
    over(0, yl, finish)

    for k, slots in ((1, (2, 3)), (-1, (4, 5))):
        @pl.when(has[k])
        def _(slots=slots):
            for slot in slots:
                for j in range(G):
                    first(j, slot, False).wait_send()
    for slot in (0, 1):
        for j in range(1, G):
            first(j, slot, False).wait_send()
    sent(*[name for name in later if not name.startswith("x_")])


def local(G, D, forcing, viscosity):
    _, xl, yl, Z = forcing.shape
    X = G * xl
    assert yl == 16 and xl % 4 == 0 and D > NEAR
    rows0, rows1, rows2 = yl + 2 * H0, yl // 4 + 2 * H1, 1 + 2 * NEAR
    f32 = jnp.float32
    vm = lambda *shape: pltpu.VMEM(shape, f32)
    sem = pltpu.SemaphoreType.DMA
    out = jax.ShapeDtypeStruct((4, yl, X, Z), f32)
    field = lambda rows: vm(4, rows, X, Z)
    any_spec = pl.BlockSpec(memory_space=pl.ANY)
    vmem_spec = pl.BlockSpec(memory_space=pltpu.VMEM)
    solved, left = pl.pallas_call(
        functools.partial(kernel, G, D, yl, xl, Z),
        out_shape=(out, out),
        in_specs=[any_spec, any_spec],
        out_specs=(vmem_spec, vmem_spec),
        scratch_shapes=[
            vm(G, 4, yl + 2 * HF, xl, Z), vm(G, yl + 2 * HV, xl, Z),
            vm(rows0, X, Z), field(rows0), field(rows0), field(rows0), vm(9, rows0, X, Z),
            vm(rows1, X, Z), field(rows1), field(rows1), field(rows1), vm(9, rows1, X, Z),
            vm(rows2, X, Z), field(rows2), field(rows2), field(rows2), vm(9, rows2, X, Z),
            vm(2, 2, X, Z), vm(2, 2, X, Z), vm(2, X, Z),
            vm(2, 2, 2, X, Z), vm(2, 2, 2, X, Z),
            vm(2, 2, 2, X, Z), vm(2, 2, 2, X, Z),
            vm(X, Z), vm(4, X, Z),
            sem((2,)), sem((G, 6)), sem((G, 6)), sem((14,)), sem((14,)),
        ],
        compiler_params=pltpu.CompilerParams(
            collective_id=0, has_side_effects=True, vmem_limit_bytes=50 * 1024 * 1024),
    )(jnp.transpose(forcing, (0, 2, 1, 3)), jnp.transpose(viscosity, (1, 0, 2)))
    at = lax.axis_index("grp") * xl

    def mine(array):
        part = lax.dynamic_slice_in_dim(array, at, xl, 2)
        return jnp.transpose(part, (0, 2, 1, 3))

    return mine(solved), mine(left)


def solution(mesh):
    G, D = mesh.shape["grp"], mesh.shape["dev"]
    in_specs = (P(None, "grp", "dev", None), P("grp", "dev", None))
    out_specs = (P(None, "grp", "dev", None), P(None, "grp", "dev", None))
    return jax.shard_map(
        functools.partial(local, G, D), mesh=mesh, in_specs=in_specs, out_specs=out_specs,
        check_vma=False)
```

```python
import functools

import jax
import jax.numpy as jnp
from jax import lax
from jax.experimental import pallas as pl
from jax.experimental.pallas import tpu as pltpu
from jax.sharding import PartitionSpec as P

OMEGA = 0.6
BETA = 0.25
COARSE = 6
MESH = pl.DeviceIdType.MESH

H0, H1 = 3, 2
HF, HV = 2, 3
NEAR = 2


def over(lo, hi, body, most=10):
    count = hi - lo
    steps = -(-count // most)
    while count % steps:
        steps += 1
    block = count // steps

    def step(i, carry):
        for j in range(block):
            body(lo + i * block + j)
        return carry

    if steps == 1:
        step(0, 0)
    else:
        lax.fori_loop(0, steps, step, 0)


def kernel(G, D, yl, xl, Z, f_in, v_in, x_out, r_out,
           FR, VR, RF, RV, E0, B0, U0a, U0b, C0, E1, B1, U1a, U1b, C1, E2, B2, U2a, U2b, C2,
           EPs, EPr, EP2r, QBs, QBr, QYs, QYr, QZs, QZr,
           local_sem, s1, r1, s2, r2):
    X = G * xl
    n1 = yl // 4
    g = lax.axis_index("grp")
    d = lax.axis_index("dev")
    f32 = jnp.float32

    own_f = pltpu.make_async_copy(f_in, FR, local_sem.at[0])
    own_v = pltpu.make_async_copy(v_in, VR, local_sem.at[1])
    own_v.start()
    own_f.start()

    barrier = pltpu.get_barrier_semaphore()
    has = {k: jnp.logical_and(d + k >= 0, d + k < D) for k in (-2, -1, 1, 2)}
    expected = G - 1
    for j in range(1, G):
        pl.semaphore_signal(barrier, inc=1, device_id=(lax.rem(g + j, G), d), device_id_type=MESH)
    for k in (-1, 1):
        @pl.when(has[k])
        def _(k=k):
            for j in range(G):
                pl.semaphore_signal(
                    barrier, inc=1, device_id=(lax.rem(g + j, G), d + k), device_id_type=MESH)
        expected = expected + G * has[k].astype(jnp.int32)
    for k in (-2, 2):
        @pl.when(has[k])
        def _(k=k):
            pl.semaphore_signal(barrier, inc=1, device_id=(g, d + k), device_id_type=MESH)
        expected = expected + has[k].astype(jnp.int32)

    @pl.when(d == 0)
    def _():
        RV[:, 0:HV] = jnp.zeros((G, HV, xl, Z), f32)
        RF[:, :, 0:HF] = jnp.zeros((G, 4, HF, xl, Z), f32)
        U0b[:, 0:2] = jnp.zeros((4, 2, X, Z), f32)
        EPr[0] = jnp.zeros((2, X, Z), f32)
        QBr[0] = jnp.zeros((2, 2, X, Z), f32)
        QYr[0] = jnp.zeros((2, 2, X, Z), f32)
        QZr[1] = jnp.zeros((X, Z), f32)

    @pl.when(d < 2)
    def _():
        EP2r[0] = jnp.zeros((X, Z), f32)
        QZr[0] = jnp.zeros((X, Z), f32)

    @pl.when(d == D - 1)
    def _():
        RV[:, HV + yl:] = jnp.zeros((G, HV, xl, Z), f32)
        RF[:, :, HF + yl:] = jnp.zeros((G, 4, HF, xl, Z), f32)
        U0b[:, yl + 4:] = jnp.zeros((4, 2, X, Z), f32)
        EPr[1] = jnp.zeros((2, X, Z), f32)
        QBr[1] = jnp.zeros((2, 2, X, Z), f32)
        QYr[1] = jnp.zeros((2, 2, X, Z), f32)
        QZr[2] = jnp.zeros((X, Z), f32)

    @pl.when(d >= D - 2)
    def _():
        EP2r[1] = jnp.zeros((X, Z), f32)
        QZr[3] = jnp.zeros((X, Z), f32)

    def planes(c, y, h):
        start = c * xl * yl * (Z // 128) + (y // 8) * 8 * (Z // 128) + h * 8 + y % 8
        return pl.ds(start, xl, stride=yl * (Z // 128))

    own_v.wait()
    for y in range(yl):
        for h in range(Z // 128):
            RV[g, HV + y, :, h * 128:(h + 1) * 128] = VR[planes(0, y, h), :]
    own_f.wait()
    for c in range(4):
        for y in range(yl):
            for h in range(Z // 128):
                RF[g, c, HF + y, :, h * 128:(h + 1) * 128] = FR[planes(c, y, h), :]

    pl.semaphore_wait(barrier, expected)

    def rdma(src, dst, ss, rs, target):
        return pltpu.make_async_remote_copy(
            src_ref=src, dst_ref=dst, send_sem=ss, recv_sem=rs,
            device_id=target, device_id_type=MESH)

    def first(j, slot, source):
        other = lax.rem(g + j, G)
        at = other if source else g
        k = (0, 0, 1, 1, -1, -1)[slot]
        if slot % 2 == 0:
            rows, put = {0: (0, HV), 1: (yl - HV, 0), -1: (0, HV + yl)}[k]
            count = yl if k == 0 else HV
            src, dst = RV.at[g, pl.ds(HV + rows, count)], RV.at[at, pl.ds(put, count)]
        else:
            rows, put = {0: (0, HF), 1: (yl - HF, 0), -1: (0, HF + yl)}[k]
            count = yl if k == 0 else HF
            src, dst = RF.at[g, :, pl.ds(HF + rows, count)], RF.at[at, :, pl.ds(put, count)]
        return rdma(src, dst, s1.at[j, slot], r1.at[at, slot], (other, d + k))

    for k, slots in ((1, (2, 3)), (-1, (4, 5))):
        @pl.when(has[k])
        def _(slots=slots):
            for slot in slots:
                for j in range(G):
                    first(j, slot, False).start()
    for slot in (0, 1):
        for j in range(1, G):
            first(j, slot, False).start()

    lo1, hi1 = H1, H1 + n1
    later = {
        "e_up": (EPs.at[1], EPr.at[0], 1),
        "e_down": (EPs.at[0], EPr.at[1], -1),
        "e_up2": (EPs.at[1, 0], EP2r.at[0], 2),
        "e_down2": (EPs.at[0, 0], EP2r.at[1], -2),
        "b_up": (QBs.at[1], QBr.at[0], 1),
        "b_down": (QBs.at[0], QBr.at[1], -1),
        "x_up": (U0b.at[:, pl.ds(yl, 2)], U0b.at[:, pl.ds(0, 2)], 1),
        "x_down": (U0b.at[:, pl.ds(4, 2)], U0b.at[:, pl.ds(yl + 4, 2)], -1),
        "y_up": (QYs.at[1], QYr.at[0], 1),
        "y_down": (QYs.at[0], QYr.at[1], -1),
        "z_up2": (QZs, QZr.at[0], 2),
        "z_up": (QZs, QZr.at[1], 1),
        "z_down": (QZs, QZr.at[2], -1),
        "z_down2": (QZs, QZr.at[3], -2),
    }
    index_of = {name: i for i, name in enumerate(later)}

    def copy_of(name):
        src, dst, k = later[name]
        i = index_of[name]
        return rdma(src, dst, s2.at[i], r2.at[i], (g, d + k)), k

    def start(*names):
        for name in names:
            copy, k = copy_of(name)
            pl.when(has[k])(copy.start)

    def receive(*names):
        for name in names:
            copy, k = copy_of(name)
            pl.when(has[-k])(copy.wait_recv)

    def sent(*names):
        for name in names:
            copy, k = copy_of(name)
            pl.when(has[k])(copy.wait_send)

    sub = lax.broadcasted_iota(jnp.int32, (X, Z), 0)
    lane = lax.broadcasted_iota(jnp.int32, (X, Z), 1)

    def roll(value, shift, dim):
        axis = value.ndim - 2 + dim
        return pltpu.roll(value, shift % value.shape[axis], axis)

    def partner(value, s):
        value = value + jnp.where((sub & s) == 0, roll(value, -s, 0), roll(value, s, 0))
        return value + jnp.where((lane & s) == 0, roll(value, -s, 1), roll(value, s, 1))

    def spread(value, ids, dim, s):
        odd = (ids & s) != 0
        return (jnp.where(odd, roll(value, s, dim), value),
                jnp.where(odd, value, roll(value, -s, dim)))

    def pack2(c):
        return jnp.where((lane & 1) != 0, c[1], c[0])

    def unpack2(packed):
        return spread(packed, lane, 1, 1)

    def pick4(c, ids):
        a, b = (ids & 1) != 0, (ids & 2) != 0
        return jnp.where(b, jnp.where(a, c[3], c[2]), jnp.where(a, c[1], c[0]))

    def spread4(packed, ids, dim):
        even, odd = spread(packed, ids, dim, 1)
        v0, v2 = spread(even, ids, dim, 2)
        v1, v3 = spread(odd, ids, dim, 2)
        return [v0, v1, v2, v3]

    def next_of(get, i, s, last):
        if s == 1:
            return get(i + 1)
        return jnp.where((sub & (s - 1)) == s - 1,
                         roll(get(min(i + 1, last)), s - 1, 0), roll(get(i), -1, 0))

    def prev_of(get, i, s, last):
        if s == 1:
            return get(i - 1)
        return jnp.where((sub & (s - 1)) == 0,
                         roll(get(max(i - 1, 0)), 1 - s, 0), roll(get(i), 1, 0))

    def level(s, E, B, C):
        last = E.shape[0] - 1
        inside = ((sub < X - s), (sub >= s), (lane < Z - s), (lane >= s))
        half = [jnp.where(m, f32(0.5 / s), f32(0.0)) for m in inside]
        scale = 1.0 / (s * s)

        def coefficients(lo, hi):
            def body(r):
                e = E[r]
                xs = [jnp.where(m, roll(e, sh, dim), 0.0)
                      for m, sh, dim in zip(inside, (-s, s, -s, s), (0, 0, 1, 1))]
                get = lambda i: E[i]
                ys = [next_of(get, r, s, last), prev_of(get, r, s, last)]
                fx = [(e + other) * (0.5 * scale) for other in xs]
                fy = [(e + other) * (0.5 * scale) for other in ys]
                diagonal = (fx[0] + fx[1]) + (fy[0] + fy[1]) + (fx[2] + fx[3])
                for i in range(4):
                    C[i, r] = jnp.where(inside[i], fx[i], 0.0)
                C[4, r] = fy[0]
                C[5, r] = fy[1]
                real = e > 0.0
                C[6, r] = jnp.where(real, OMEGA / jnp.where(real, diagonal, 1.0), 0.0)
                C[7, r] = BETA * e
                C[8, r] = diagonal
            over(lo, hi, body)

        def begin(U, lo, hi):
            def body(r):
                w = C[6, r]
                for c in range(3):
                    U[c, r] = w * B[c, r]
                U[3, r] = C[7, r] * B[3, r]
            over(lo, hi, body)

        def parts(U, r):
            coef = [C[i, r] for i in range(6)]
            centre = [U[c, r] for c in range(4)]
            rolled = []
            for c in range(4):
                u = centre[c]
                rolled.append([roll(u, -s, 0), roll(u, s, 0), roll(u, -s, 1), roll(u, s, 1),
                               next_of(lambda i: U[c, i], r, s, last),
                               prev_of(lambda i: U[c, i], r, s, last)])
            p = rolled[3]
            grad = [half[0] * p[0] - half[1] * p[1], (p[4] - p[5]) * (0.5 / s),
                    half[2] * p[2] - half[3] * p[3]]
            out = []
            for c in range(3):
                t = [coef[i] * rolled[c][i] for i in range(6)]
                total = (t[0] + t[1]) + (t[2] + t[3]) + (t[4] + t[5])
                out.append((B[c, r] - grad[c]) + total)
            div = ((half[0] * rolled[0][0] - half[1] * rolled[0][1])
                   + (rolled[1][4] - rolled[1][5]) * (0.5 / s)
                   + (half[2] * rolled[2][2] - half[3] * rolled[2][3]))
            out.append(B[3, r] - div)
            return centre, out

        def sweep(U, V, lo, hi, also=None):
            def body(r):
                centre, out = parts(U, r)
                w = C[6, r]
                for c in range(3):
                    V[c, r] = (1.0 - OMEGA) * centre[c] + w * out[c]
                V[3, r] = centre[3] + C[7, r] * out[3]
            over(lo, hi, body)

        def residual(U, r):
            centre, out = parts(U, r)
            diagonal = C[8, r]
            return [out[c] - diagonal * centre[c] for c in range(3)] + [out[3]]

        return coefficients, begin, sweep, residual

    def restrict0(rows):
        return jnp.where((sub & 1) == 0, partner(rows[0] + rows[1], 1),
                         partner(rows[2] + rows[3], 1)) * 0.125

    def restrict1(tile):
        tile = tile + jnp.where((sub & 1) == 0, roll(tile, -1, 0), roll(tile, 1, 0))
        return partner(tile, 2) * 0.125

    coef0, begin0, sweep0, res0 = level(1, E0, B0, C0)
    coef1, begin1, sweep1, res1 = level(2, E1, B1, C1)
    coef2, begin2, sweep2, res2 = level(4, E2, B2, C2)

    def place_v(lo, hi):
        for i in range(G):
            E0[lo:hi, i * xl:(i + 1) * xl, :] = RV[i, lo:hi]

    def place_f(lo, hi):
        for i in range(G):
            for c in range(4):
                B0[c, lo + H0 - HF:hi + H0 - HF, i * xl:(i + 1) * xl, :] = RF[i, c, lo:hi]

    for j in range(1, G):
        first(j, 0, True).wait_recv()
    place_v(HV, HV + yl)

    def coarse_e(r):
        E1[lo1 + r] = restrict0([E0[H0 + 4 * r + i] for i in range(4)])
    over(0, n1, coarse_e)
    packed = pick4([restrict1(E1[lo1 + i]) for i in range(n1)], sub)
    E2[NEAR] = packed
    EPs[0, 0] = packed
    EPs[1, 0] = packed
    EPs[0, 1] = pack2([E1[lo1], E1[lo1 + 1]])
    EPs[1, 1] = pack2([E1[hi1 - 2], E1[hi1 - 1]])
    start("e_up", "e_down", "e_up2", "e_down2")

    for j in range(1, G):
        first(j, 1, True).wait_recv()
    place_f(HF, HF + yl)
    top, end = H0, H0 + yl
    coef0(top + 1, end - 1)
    begin0(U0a, top + 1, end - 1)
    sweep0(U0a, U0b, top + 2, end - 2)

    for k, slots in ((1, (2, 3)), (-1, (4, 5))):
        @pl.when(has[-k])
        def _(slots=slots):
            for slot in slots:
                for j in range(G):
                    first(j, slot, True).wait_recv()
    for a, b in ((0, HV), (HV + yl, 2 * HV + yl)):
        place_v(a, b)
    for a, b in ((0, HF), (HF + yl, 2 * HF + yl)):
        place_f(a, b)
    for a, b in ((top - 2, top + 1), (end - 1, end + 2)):
        coef0(a, b)
        begin0(U0a, a, b)
    for a, b in ((top - 1, top + 2), (end - 2, end + 1)):
        sweep0(U0a, U0b, a, b)

    def coarse_b(r):
        rows = [res0(U0b, H0 + 4 * r + i) for i in range(4)]
        for c in range(4):
            B1[c, lo1 + r] = restrict0([row[c] for row in rows])
    over(0, n1, coarse_b, 2)

    def pack_tiles(packed, U):
        for i in range(2):
            for half in range(2):
                pair = (2 * half, 2 * half + 1)
                packed[0, i, half] = pack2([U[c, lo1 + i] for c in pair])
                packed[1, i, half] = pack2([U[c, hi1 - 2 + i] for c in pair])

    def unpack_tiles(packed, U):
        for i in range(2):
            for half in range(2):
                for side, at in ((0, lo1 - 2), (1, hi1)):
                    for c, value in enumerate(unpack2(packed[side, i, half])):
                        U[2 * half + c, at + i] = value

    pack_tiles(QBs, B1)
    start("b_up", "b_down")

    receive("e_up", "e_down", "e_up2", "e_down2")
    for i in range(2):
        E1[i] = unpack2(EPr[0, 1])[i]
        E1[hi1 + i] = unpack2(EPr[1, 1])[i]
    for at, value in ((0, EP2r[0]), (1, EPr[0, 0]), (3, EPr[1, 0]), (4, EP2r[1])):
        E2[at] = value
    coef1(0, hi1 + 2)
    coef2(0, 2 * NEAR + 1)
    begin1(U1a, lo1, hi1)
    receive("b_up", "b_down")
    unpack_tiles(QBr, B1)
    begin1(U1a, lo1 - 2, lo1)
    begin1(U1a, hi1, hi1 + 2)
    sweep1(U1a, U1b, lo1 - 1, hi1 + 1)
    rows = []
    for i in range(n1):
        rows.append([restrict1(value) for value in res1(U1b, lo1 + i)])
    for c in range(4):
        B2[c, NEAR] = pick4([row[c] for row in rows], sub)
    QZs[...] = pick4([B2[c, NEAR] for c in range(4)], lane)
    start("z_up2", "z_down2", "z_up", "z_down")
    pack_tiles(QYs, U1b)
    start("y_up", "y_down", "x_up", "x_down")

    begin2(U2a, NEAR, NEAR + 1)
    receive("z_up2", "z_up", "z_down", "z_down2")
    for slot, at in enumerate((0, 1, 3, 4)):
        for c, field in enumerate(spread4(QZr[slot], lane, 1)):
            B2[c, at] = field
    begin2(U2a, 0, NEAR)
    begin2(U2a, NEAR + 1, 2 * NEAR + 1)
    here, there = U2a, U2b
    for i in range(COARSE - 1):
        sweep2(here, there, 0, 2 * NEAR + 1)
        here, there = there, here

    receive("y_up", "y_down")
    unpack_tiles(QYr, U1b)
    for c in range(4):
        below, own, above = [spread4(here[c, i], sub, 0) for i in (1, 2, 3)]
        for i, z in enumerate(below[2:] + own + above[:2]):
            U1b[c, i] = U1b[c, i] + z
    sweep1(U1b, U1a, 0, hi1 + 2)
    sweep1(U1a, U1b, lo1 - 1, hi1 + 1)

    receive("x_up", "x_down")
    sent("x_up", "x_down")

    def add0(r):
        for c in range(4):
            for i, y in enumerate(spread(U1b[c, lo1 + r], sub, 0, 1)):
                for at in (H0 + 4 * r + 2 * i, H0 + 4 * r + 2 * i + 1):
                    U0b[c, at] = U0b[c, at] + y
    over(0, n1, add0, 2)
    for c in range(4):
        low = spread(U1b[c, lo1 - 1], sub, 0, 1)
        high = spread(U1b[c, hi1], sub, 0, 1)
        for at, y in ((0, low[0]), (1, low[1]), (2, low[1]),
                      (yl + 3, high[0]), (yl + 4, high[0]), (yl + 5, high[1])):
            U0b[c, at] = U0b[c, at] + y
    sweep0(U0b, U0a, top - 2, end + 2)
    sweep0(U0a, U0b, top - 1, end + 1)

    def own_planes(value):
        kept = value[:xl]
        for i in range(1, G):
            kept = jnp.where(g == i, value[i * xl:(i + 1) * xl], kept)
        return kept

    def finish(r):
        for c, value in enumerate(res0(U0b, H0 + r)):
            kept = own_planes(U0b[c, H0 + r]), own_planes(value)
            for h in range(Z // 128):
                x_out[planes(c, r, h), :] = kept[0][:, h * 128:(h + 1) * 128]
                r_out[planes(c, r, h), :] = kept[1][:, h * 128:(h + 1) * 128]
    over(0, yl, finish)

    for k, slots in ((1, (2, 3)), (-1, (4, 5))):
        @pl.when(has[k])
        def _(slots=slots):
            for slot in slots:
                for j in range(G):
                    first(j, slot, False).wait_send()
    for slot in (0, 1):
        for j in range(1, G):
            first(j, slot, False).wait_send()
    sent(*[name for name in later if not name.startswith("x_")])


def tiles(array):
    Z = array.shape[-1]
    return jnp.swapaxes(array.reshape(-1, 8, Z // 128, 128), 1, 2).reshape(-1, 128)


def local(G, D, forcing, viscosity):
    _, xl, yl, Z = forcing.shape
    X = G * xl
    assert yl == 16 and xl % 4 == 0 and D > NEAR
    rows0, rows1, rows2 = yl + 2 * H0, yl // 4 + 2 * H1, 1 + 2 * NEAR
    f32 = jnp.float32
    vm = lambda *shape: pltpu.VMEM(shape, f32)
    sem = pltpu.SemaphoreType.DMA
    out = jax.ShapeDtypeStruct((4 * xl * yl * (Z // 128), 128), f32)
    field = lambda rows: vm(4, rows, X, Z)
    any_spec = pl.BlockSpec(memory_space=pl.ANY)
    vmem_spec = pl.BlockSpec(memory_space=pltpu.VMEM)
    solved, left = pl.pallas_call(
        functools.partial(kernel, G, D, yl, xl, Z),
        out_shape=(out, out),
        in_specs=[any_spec, any_spec],
        out_specs=(vmem_spec, vmem_spec),
        scratch_shapes=[
            vm(4 * xl * yl * (Z // 128), 128), vm(xl * yl * (Z // 128), 128),
            vm(G, 4, yl + 2 * HF, xl, Z), vm(G, yl + 2 * HV, xl, Z),
            vm(rows0, X, Z), field(rows0), field(rows0), field(rows0), vm(9, rows0, X, Z),
            vm(rows1, X, Z), field(rows1), field(rows1), field(rows1), vm(9, rows1, X, Z),
            vm(rows2, X, Z), field(rows2), field(rows2), field(rows2), vm(9, rows2, X, Z),
            vm(2, 2, X, Z), vm(2, 2, X, Z), vm(2, X, Z),
            vm(2, 2, 2, X, Z), vm(2, 2, 2, X, Z),
            vm(2, 2, 2, X, Z), vm(2, 2, 2, X, Z),
            vm(X, Z), vm(4, X, Z),
            sem((2,)), sem((G, 6)), sem((G, 6)), sem((14,)), sem((14,)),
        ],
        compiler_params=pltpu.CompilerParams(
            collective_id=0, has_side_effects=True, vmem_limit_bytes=50 * 1024 * 1024),
    )(tiles(forcing), tiles(viscosity))

    def whole(array):
        array = array.reshape(4 * xl * yl // 8, Z // 128, 8, 128)
        return jnp.swapaxes(array, 1, 2).reshape(forcing.shape)

    return whole(solved), whole(left)


def solution(mesh):
    G, D = mesh.shape["grp"], mesh.shape["dev"]
    in_specs = (P(None, "grp", "dev", None), P("grp", "dev", None))
    out_specs = (P(None, "grp", "dev", None), P(None, "grp", "dev", None))
    return jax.shard_map(
        functools.partial(local, G, D), mesh=mesh, in_specs=in_specs, out_specs=out_specs,
        check_vma=False)
```

```python
import functools

import jax
import jax.numpy as jnp
from jax import lax
from jax.experimental import pallas as pl
from jax.experimental.pallas import tpu as pltpu
from jax.sharding import PartitionSpec as P

OMEGA = 0.6
BETA = 0.25
COARSE = 6
MESH = pl.DeviceIdType.MESH

H0, H1 = 3, 2
HF, HV = 2, 3
GRANT = 64768 * 1024
NEAR = 2


def over(lo, hi, body, most=10):
    count = hi - lo
    steps = -(-count // most)
    while count % steps:
        steps += 1
    block = count // steps

    def step(i, carry):
        for j in range(block):
            body(lo + i * block + j)
        return carry

    if steps == 1:
        step(0, 0)
    else:
        lax.fori_loop(0, steps, step, 0)


def kernel(G, D, yl, xl, Z, f_in, v_in, x_out, r_out,
           XO, RO, FR, VR, RF, RV, E0, B0, U0a, U0b, C0, E1, B1, U1a, U1b, C1, E2, B2, U2a, U2b, C2,
           EPs, EPr, EP2r, QBs, QBr, QYs, QYr, QZs, QZr,
           local_sem, s1, r1, s2, r2):
    X = G * xl
    n1 = yl // 4
    g = lax.axis_index("grp")
    d = lax.axis_index("dev")
    f32 = jnp.float32

    own_f = pltpu.make_async_copy(f_in, FR, local_sem.at[0])
    own_v = pltpu.make_async_copy(v_in, VR, local_sem.at[1])
    own_v.start()
    own_f.start()

    barrier = pltpu.get_barrier_semaphore()
    has = {k: jnp.logical_and(d + k >= 0, d + k < D) for k in (-2, -1, 1, 2)}
    expected = G - 1
    for j in range(1, G):
        pl.semaphore_signal(barrier, inc=1, device_id=(lax.rem(g + j, G), d), device_id_type=MESH)
    for k in (-2, -1, 1, 2):
        @pl.when(has[k])
        def _(k=k):
            pl.semaphore_signal(barrier, inc=1, device_id=(g, d + k), device_id_type=MESH)
        expected = expected + has[k].astype(jnp.int32)

    @pl.when(d == 0)
    def _():
        RV[:, 0:HV] = jnp.zeros((G, HV, xl, Z), f32)
        RF[:, :, 0:HF] = jnp.zeros((G, 4, HF, xl, Z), f32)
        U0b[:, 0:2] = jnp.zeros((4, 2, X, Z), f32)
        EPr[0] = jnp.zeros((2, X, Z), f32)
        QBr[0] = jnp.zeros((2, 2, X, Z), f32)
        QYr[0] = jnp.zeros((2, 2, X, Z), f32)
        QZr[1] = jnp.zeros((X, Z), f32)

    @pl.when(d < 2)
    def _():
        EP2r[0] = jnp.zeros((X, Z), f32)
        QZr[0] = jnp.zeros((X, Z), f32)

    @pl.when(d == D - 1)
    def _():
        RV[:, HV + yl:] = jnp.zeros((G, HV, xl, Z), f32)
        RF[:, :, HF + yl:] = jnp.zeros((G, 4, HF, xl, Z), f32)
        U0b[:, yl + 4:] = jnp.zeros((4, 2, X, Z), f32)
        EPr[1] = jnp.zeros((2, X, Z), f32)
        QBr[1] = jnp.zeros((2, 2, X, Z), f32)
        QYr[1] = jnp.zeros((2, 2, X, Z), f32)
        QZr[2] = jnp.zeros((X, Z), f32)

    @pl.when(d >= D - 2)
    def _():
        EP2r[1] = jnp.zeros((X, Z), f32)
        QZr[3] = jnp.zeros((X, Z), f32)

    def planes(c, y, h):
        start = c * xl * yl * (Z // 128) + (y // 8) * 8 * (Z // 128) + h * 8 + y % 8
        return pl.ds(start, xl, stride=yl * (Z // 128))

    own_v.wait()
    for y in range(yl):
        for h in range(Z // 128):
            RV[g, HV + y, :, h * 128:(h + 1) * 128] = VR[planes(0, y, h), :]
    own_f.wait()
    for c in range(4):
        for y in range(yl):
            for h in range(Z // 128):
                RF[g, c, HF + y, :, h * 128:(h + 1) * 128] = FR[planes(c, y, h), :]

    pl.semaphore_wait(barrier, expected)

    def rdma(src, dst, ss, rs, target):
        return pltpu.make_async_remote_copy(
            src_ref=src, dst_ref=dst, send_sem=ss, recv_sem=rs,
            device_id=target, device_id_type=MESH)

    halo = ((1, (2, 3)), (-1, (4, 5)))

    def first(j, slot, source):
        other = lax.rem(g + j, G)
        at = other if source else g
        k = (0, 0, 1, 1, -1, -1)[slot]
        width = HF if slot % 2 else HV
        put = {0: width, 1: 0, -1: width + yl}[k]
        count = yl if k == 0 else width
        rows = put if j else {1: yl, -1: width}[k]
        if slot % 2:
            src, dst = RF.at[g, :, pl.ds(rows, count)], RF.at[at, :, pl.ds(put, count)]
        else:
            src, dst = RV.at[g, pl.ds(rows, count)], RV.at[at, pl.ds(put, count)]
        target = (other, d) if j else (g, d + k)
        return rdma(src, dst, s1.at[j, slot], r1.at[at, slot], target)

    for k, slots in halo:
        @pl.when(has[k])
        def _(slots=slots):
            for slot in slots:
                first(0, slot, False).start()
    for slot in (0, 1):
        for j in range(1, G):
            first(j, slot, False).start()

    lo1, hi1 = H1, H1 + n1
    later = {
        "e_up": (EPs.at[1], EPr.at[0], 1),
        "e_down": (EPs.at[0], EPr.at[1], -1),
        "e_up2": (EPs.at[1, 0], EP2r.at[0], 2),
        "e_down2": (EPs.at[0, 0], EP2r.at[1], -2),
        "b_up": (QBs.at[1], QBr.at[0], 1),
        "b_down": (QBs.at[0], QBr.at[1], -1),
        "x_up": (U0b.at[:, pl.ds(yl, 2)], U0b.at[:, pl.ds(0, 2)], 1),
        "x_down": (U0b.at[:, pl.ds(4, 2)], U0b.at[:, pl.ds(yl + 4, 2)], -1),
        "y_up": (QYs.at[1], QYr.at[0], 1),
        "y_down": (QYs.at[0], QYr.at[1], -1),
        "z_up2": (QZs, QZr.at[0], 2),
        "z_up": (QZs, QZr.at[1], 1),
        "z_down": (QZs, QZr.at[2], -1),
        "z_down2": (QZs, QZr.at[3], -2),
    }
    index_of = {name: i for i, name in enumerate(later)}

    def copy_of(name):
        src, dst, k = later[name]
        i = index_of[name]
        return rdma(src, dst, s2.at[i], r2.at[i], (g, d + k)), k

    def start(*names):
        for name in names:
            copy, k = copy_of(name)
            pl.when(has[k])(copy.start)

    def receive(*names):
        for name in names:
            copy, k = copy_of(name)
            pl.when(has[-k])(copy.wait_recv)

    def sent(*names):
        for name in names:
            copy, k = copy_of(name)
            pl.when(has[k])(copy.wait_send)

    sub = lax.broadcasted_iota(jnp.int32, (X, Z), 0)
    lane = lax.broadcasted_iota(jnp.int32, (X, Z), 1)

    def roll(value, shift, dim):
        axis = value.ndim - 2 + dim
        return pltpu.roll(value, shift % value.shape[axis], axis)

    def partner(value, s):
        value = value + jnp.where((sub & s) == 0, roll(value, -s, 0), roll(value, s, 0))
        return value + jnp.where((lane & s) == 0, roll(value, -s, 1), roll(value, s, 1))

    def spread(value, ids, dim, s):
        odd = (ids & s) != 0
        return (jnp.where(odd, roll(value, s, dim), value),
                jnp.where(odd, value, roll(value, -s, dim)))

    def pack2(c):
        return jnp.where((lane & 1) != 0, c[1], c[0])

    def unpack2(packed):
        return spread(packed, lane, 1, 1)

    def pick4(c, ids):
        a, b = (ids & 1) != 0, (ids & 2) != 0
        return jnp.where(b, jnp.where(a, c[3], c[2]), jnp.where(a, c[1], c[0]))

    def spread4(packed, ids, dim):
        even, odd = spread(packed, ids, dim, 1)
        v0, v2 = spread(even, ids, dim, 2)
        v1, v3 = spread(odd, ids, dim, 2)
        return [v0, v1, v2, v3]

    def next_of(get, i, s, last):
        if s == 1:
            return get(i + 1)
        return jnp.where((sub & (s - 1)) == s - 1,
                         roll(get(min(i + 1, last)), s - 1, 0), roll(get(i), -1, 0))

    def prev_of(get, i, s, last):
        if s == 1:
            return get(i - 1)
        return jnp.where((sub & (s - 1)) == 0,
                         roll(get(max(i - 1, 0)), 1 - s, 0), roll(get(i), 1, 0))

    def level(s, E, B, C):
        last = E.shape[0] - 1
        inside = ((sub < X - s), (sub >= s), (lane < Z - s), (lane >= s))
        half = [jnp.where(m, f32(0.5 / s), f32(0.0)) for m in inside]
        scale = 1.0 / (s * s)

        def coefficients(lo, hi):
            def body(r):
                e = E[r]
                xs = [jnp.where(m, roll(e, sh, dim), 0.0)
                      for m, sh, dim in zip(inside, (-s, s, -s, s), (0, 0, 1, 1))]
                get = lambda i: E[i]
                ys = [next_of(get, r, s, last), prev_of(get, r, s, last)]
                fx = [(e + other) * (0.5 * scale) for other in xs]
                fy = [(e + other) * (0.5 * scale) for other in ys]
                diagonal = (fx[0] + fx[1]) + (fy[0] + fy[1]) + (fx[2] + fx[3])
                for i in range(4):
                    C[i, r] = jnp.where(inside[i], fx[i], 0.0)
                C[4, r] = fy[0]
                C[5, r] = fy[1]
                real = e > 0.0
                C[6, r] = jnp.where(real, OMEGA / jnp.where(real, diagonal, 1.0), 0.0)
                C[7, r] = BETA * e
                C[8, r] = diagonal
            over(lo, hi, body)

        def begin(U, lo, hi):
            def body(r):
                w = C[6, r]
                for c in range(3):
                    U[c, r] = w * B[c, r]
                U[3, r] = C[7, r] * B[3, r]
            over(lo, hi, body)

        def parts(U, r):
            coef = [C[i, r] for i in range(6)]
            centre = [U[c, r] for c in range(4)]
            rolled = []
            for c in range(4):
                u = centre[c]
                rolled.append([roll(u, -s, 0), roll(u, s, 0), roll(u, -s, 1), roll(u, s, 1),
                               next_of(lambda i: U[c, i], r, s, last),
                               prev_of(lambda i: U[c, i], r, s, last)])
            p = rolled[3]
            grad = [half[0] * p[0] - half[1] * p[1], (p[4] - p[5]) * (0.5 / s),
                    half[2] * p[2] - half[3] * p[3]]
            out = []
            for c in range(3):
                t = [coef[i] * rolled[c][i] for i in range(6)]
                total = (t[0] + t[1]) + (t[2] + t[3]) + (t[4] + t[5])
                out.append((B[c, r] - grad[c]) + total)
            div = ((half[0] * rolled[0][0] - half[1] * rolled[0][1])
                   + (rolled[1][4] - rolled[1][5]) * (0.5 / s)
                   + (half[2] * rolled[2][2] - half[3] * rolled[2][3]))
            out.append(B[3, r] - div)
            return centre, out

        def sweep(U, V, lo, hi, also=None):
            def body(r):
                centre, out = parts(U, r)
                w = C[6, r]
                for c in range(3):
                    V[c, r] = (1.0 - OMEGA) * centre[c] + w * out[c]
                V[3, r] = centre[3] + C[7, r] * out[3]
            over(lo, hi, body)

        def residual(U, r):
            centre, out = parts(U, r)
            diagonal = C[8, r]
            return [out[c] - diagonal * centre[c] for c in range(3)] + [out[3]]

        return coefficients, begin, sweep, residual

    def restrict0(rows):
        return jnp.where((sub & 1) == 0, partner(rows[0] + rows[1], 1),
                         partner(rows[2] + rows[3], 1)) * 0.125

    def restrict1(tile):
        tile = tile + jnp.where((sub & 1) == 0, roll(tile, -1, 0), roll(tile, 1, 0))
        return partner(tile, 2) * 0.125

    coef0, begin0, sweep0, res0 = level(1, E0, B0, C0)
    coef1, begin1, sweep1, res1 = level(2, E1, B1, C1)
    coef2, begin2, sweep2, res2 = level(4, E2, B2, C2)

    def place_v(lo, hi):
        for i in range(G):
            E0[lo:hi, i * xl:(i + 1) * xl, :] = RV[i, lo:hi]

    def place_f(lo, hi):
        for i in range(G):
            for c in range(4):
                B0[c, lo + H0 - HF:hi + H0 - HF, i * xl:(i + 1) * xl, :] = RF[i, c, lo:hi]

    def hand_on():
        for k, slots in halo:
            @pl.when(has[-k])
            def _(slots=slots):
                for slot in slots:
                    first(0, slot, True).wait_recv()
                    for j in range(1, G):
                        first(j, slot, False).start()

    for j in range(1, G):
        first(j, 0, True).wait_recv()
    place_v(HV, HV + yl)

    def coarse_e(r):
        E1[lo1 + r] = restrict0([E0[H0 + 4 * r + i] for i in range(4)])
    over(0, n1, coarse_e)
    packed = pick4([restrict1(E1[lo1 + i]) for i in range(n1)], sub)
    E2[NEAR] = packed
    EPs[0, 0] = packed
    EPs[1, 0] = packed
    EPs[0, 1] = pack2([E1[lo1], E1[lo1 + 1]])
    EPs[1, 1] = pack2([E1[hi1 - 2], E1[hi1 - 1]])
    start("e_up", "e_down", "e_up2", "e_down2")

    for j in range(1, G):
        first(j, 1, True).wait_recv()
    place_f(HF, HF + yl)
    top, end = H0, H0 + yl
    coef0(top + 1, end - 1)
    begin0(U0a, top + 1, end - 1)
    hand_on()
    sweep0(U0a, U0b, top + 2, end - 2)

    for k, slots in halo:
        @pl.when(has[-k])
        def _(slots=slots):
            for slot in slots:
                for j in range(1, G):
                    first(j, slot, True).wait_recv()
    for a, b in ((0, HV), (HV + yl, 2 * HV + yl)):
        place_v(a, b)
    for a, b in ((0, HF), (HF + yl, 2 * HF + yl)):
        place_f(a, b)
    for a, b in ((top - 2, top + 1), (end - 1, end + 2)):
        coef0(a, b)
        begin0(U0a, a, b)
    for a, b in ((top - 1, top + 2), (end - 2, end + 1)):
        sweep0(U0a, U0b, a, b)

    def coarse_b(r):
        rows = [res0(U0b, H0 + 4 * r + i) for i in range(4)]
        for c in range(4):
            B1[c, lo1 + r] = restrict0([row[c] for row in rows])
    over(0, n1, coarse_b, 2)

    def pack_tiles(packed, U):
        for i in range(2):
            for half in range(2):
                pair = (2 * half, 2 * half + 1)
                packed[0, i, half] = pack2([U[c, lo1 + i] for c in pair])
                packed[1, i, half] = pack2([U[c, hi1 - 2 + i] for c in pair])

    def unpack_tiles(packed, U):
        for i in range(2):
            for half in range(2):
                for side, at in ((0, lo1 - 2), (1, hi1)):
                    for c, value in enumerate(unpack2(packed[side, i, half])):
                        U[2 * half + c, at + i] = value

    pack_tiles(QBs, B1)
    start("b_up", "b_down")

    receive("e_up", "e_down", "e_up2", "e_down2")
    for i in range(2):
        E1[i] = unpack2(EPr[0, 1])[i]
        E1[hi1 + i] = unpack2(EPr[1, 1])[i]
    for at, value in ((0, EP2r[0]), (1, EPr[0, 0]), (3, EPr[1, 0]), (4, EP2r[1])):
        E2[at] = value
    coef1(0, hi1 + 2)
    coef2(0, 2 * NEAR + 1)
    begin1(U1a, lo1, hi1)
    receive("b_up", "b_down")
    unpack_tiles(QBr, B1)
    begin1(U1a, lo1 - 2, lo1)
    begin1(U1a, hi1, hi1 + 2)
    sweep1(U1a, U1b, lo1 - 1, hi1 + 1)
    rows = []
    for i in range(n1):
        rows.append([restrict1(value) for value in res1(U1b, lo1 + i)])
    for c in range(4):
        B2[c, NEAR] = pick4([row[c] for row in rows], sub)
    QZs[...] = pick4([B2[c, NEAR] for c in range(4)], lane)
    start("z_up2", "z_down2", "z_up", "z_down")
    pack_tiles(QYs, U1b)
    start("y_up", "y_down", "x_up", "x_down")

    begin2(U2a, NEAR, NEAR + 1)
    receive("z_up2", "z_up", "z_down", "z_down2")
    for slot, at in enumerate((0, 1, 3, 4)):
        for c, field in enumerate(spread4(QZr[slot], lane, 1)):
            B2[c, at] = field
    begin2(U2a, 0, NEAR)
    begin2(U2a, NEAR + 1, 2 * NEAR + 1)
    here, there = U2a, U2b
    for i in range(COARSE - 1):
        sweep2(here, there, 0, 2 * NEAR + 1)
        here, there = there, here

    receive("y_up", "y_down")
    unpack_tiles(QYr, U1b)
    for c in range(4):
        below, own, above = [spread4(here[c, i], sub, 0) for i in (1, 2, 3)]
        for i, z in enumerate(below[2:] + own + above[:2]):
            U1b[c, i] = U1b[c, i] + z
    sweep1(U1b, U1a, 0, hi1 + 2)
    sweep1(U1a, U1b, lo1 - 1, hi1 + 1)

    receive("x_up", "x_down")
    sent("x_up", "x_down")

    def add0(r):
        for c in range(4):
            for i, y in enumerate(spread(U1b[c, lo1 + r], sub, 0, 1)):
                for at in (H0 + 4 * r + 2 * i, H0 + 4 * r + 2 * i + 1):
                    U0b[c, at] = U0b[c, at] + y
    over(0, n1, add0, 2)
    for c in range(4):
        low = spread(U1b[c, lo1 - 1], sub, 0, 1)
        high = spread(U1b[c, hi1], sub, 0, 1)
        for at, y in ((0, low[0]), (1, low[1]), (2, low[1]),
                      (yl + 3, high[0]), (yl + 4, high[0]), (yl + 5, high[1])):
            U0b[c, at] = U0b[c, at] + y
    sweep0(U0b, U0a, top - 2, end + 2)
    sweep0(U0a, U0b, top - 1, end + 1)

    def own_planes(value):
        kept = value[:xl]
        for i in range(1, G):
            kept = jnp.where(g == i, value[i * xl:(i + 1) * xl], kept)
        return kept

    def store(ref, c, r, value):
        kept = own_planes(value)
        for h in range(Z // 128):
            ref[planes(c, r, h), :] = kept[:, h * 128:(h + 1) * 128]

    def finish_x(r):
        for c in range(4):
            store(XO, c, r, U0b[c, H0 + r])
    over(0, yl, finish_x)
    put_x = pltpu.make_async_copy(XO, x_out, local_sem.at[2])
    put_x.start()

    def finish_r(r):
        for c, value in enumerate(res0(U0b, H0 + r)):
            store(RO, c, r, value)
    over(0, yl, finish_r)
    put_r = pltpu.make_async_copy(RO, r_out, local_sem.at[3])
    put_r.start()

    for k, slots in halo:
        @pl.when(has[k])
        def _(slots=slots):
            for slot in slots:
                first(0, slot, False).wait_send()

        @pl.when(has[-k])
        def _(slots=slots):
            for slot in slots:
                for j in range(1, G):
                    first(j, slot, False).wait_send()
    for slot in (0, 1):
        for j in range(1, G):
            first(j, slot, False).wait_send()
    sent(*[name for name in later if not name.startswith("x_")])
    put_x.wait()
    put_r.wait()


def write_out(x_in, r_in, x_out, r_out, sems):
    half = x_in.shape[0] // 2
    copies = [
        pltpu.make_async_copy(a.at[pl.ds(i * half, half)], b.at[pl.ds(i * half, half)], sems.at[2 * k + i])
        for k, (a, b) in enumerate(((x_in, x_out), (r_in, r_out))) for i in range(2)]
    for copy in copies:
        copy.start()
    for copy in copies:
        copy.wait()


def tiles(array):
    Z = array.shape[-1]
    return jnp.swapaxes(array.reshape(-1, 8, Z // 128, 128), 1, 2).reshape(-1, 128)


def local(G, D, forcing, viscosity):
    _, xl, yl, Z = forcing.shape
    X = G * xl
    assert yl == 16 and xl % 4 == 0 and D > NEAR
    rows0, rows1, rows2 = yl + 2 * H0, yl // 4 + 2 * H1, 1 + 2 * NEAR
    f32 = jnp.float32
    vm = lambda *shape: pltpu.VMEM(shape, f32)
    sem = pltpu.SemaphoreType.DMA
    out = jax.ShapeDtypeStruct((4 * xl * yl * (Z // 128), 128), f32)
    field = lambda rows: vm(4, rows, X, Z)
    hbm_spec = pl.BlockSpec(memory_space=pltpu.HBM)
    any_spec = pl.BlockSpec(memory_space=pl.ANY)
    solved, left = pl.pallas_call(
        functools.partial(kernel, G, D, yl, xl, Z),
        out_shape=(out, out),
        in_specs=[hbm_spec, hbm_spec],
        out_specs=(hbm_spec, hbm_spec),
        scratch_shapes=[
            *[vm(4 * xl * yl * (Z // 128), 128)] * 3, vm(xl * yl * (Z // 128), 128),
            vm(G, 4, yl + 2 * HF, xl, Z), vm(G, yl + 2 * HV, xl, Z),
            vm(rows0, X, Z), field(rows0), field(rows0), field(rows0), vm(9, rows0, X, Z),
            vm(rows1, X, Z), field(rows1), field(rows1), field(rows1), vm(9, rows1, X, Z),
            vm(rows2, X, Z), field(rows2), field(rows2), field(rows2), vm(9, rows2, X, Z),
            vm(2, 2, X, Z), vm(2, 2, X, Z), vm(2, X, Z),
            vm(2, 2, 2, X, Z), vm(2, 2, 2, X, Z),
            vm(2, 2, 2, X, Z), vm(2, 2, 2, X, Z),
            vm(X, Z), vm(4, X, Z),
            sem((4,)), sem((G, 6)), sem((G, 6)), sem((14,)), sem((14,)),
        ],
        compiler_params=pltpu.CompilerParams(
            collective_id=0, has_side_effects=True, vmem_limit_bytes=GRANT),
    )(tiles(forcing), tiles(viscosity))
    solved, left = pl.pallas_call(
        write_out,
        out_shape=(out, out),
        in_specs=[any_spec, any_spec],
        out_specs=(hbm_spec, hbm_spec),
        scratch_shapes=[sem((4,))],
        compiler_params=pltpu.CompilerParams(vmem_limit_bytes=GRANT),
    )(solved, left)

    def whole(array):
        array = array.reshape(4 * xl * yl // 8, Z // 128, 8, 128)
        return jnp.swapaxes(array, 1, 2).reshape(forcing.shape)

    return whole(solved), whole(left)


def solution(mesh):
    G, D = mesh.shape["grp"], mesh.shape["dev"]
    in_specs = (P(None, "grp", "dev", None), P("grp", "dev", None))
    out_specs = (P(None, "grp", "dev", None), P(None, "grp", "dev", None))
    return jax.shard_map(
        functools.partial(local, G, D), mesh=mesh, in_specs=in_specs, out_specs=out_specs,
        check_vma=False)
```

```python
import functools

import jax
import jax.numpy as jnp
from jax import lax
from jax.experimental import pallas as pl
from jax.experimental.pallas import tpu as pltpu
from jax.sharding import PartitionSpec as P

OMEGA = 0.6
BETA = 0.25
COARSE = 6
MESH = pl.DeviceIdType.MESH

H0, H1 = 3, 2
HF, HV = 2, 3
GRANT = 64768 * 1024
NEAR = 2


def over(lo, hi, body, most=10):
    count = hi - lo
    steps = -(-count // most)
    while count % steps:
        steps += 1
    block = count // steps

    def step(i, carry):
        for j in range(block):
            body(lo + i * block + j)
        return carry

    if steps == 1:
        step(0, 0)
    else:
        lax.fori_loop(0, steps, step, 0)


def kernel(G, D, yl, xl, Z, f_in, v_in, x_out, r_out,
           XO, RO, FR, VR, RF, RV, E0, B0, U0a, U0b, C0, E1, B1, U1a, U1b, C1, E2, B2, U2a, U2b, C2,
           EPs, EPr, EP2r, QBs, QBr, QYs, QYr, QZs, QZr,
           local_sem, s1, r1, s2, r2):
    X = G * xl
    n1 = yl // 4
    g = lax.axis_index("grp")
    d = lax.axis_index("dev")
    f32 = jnp.float32

    own_f = pltpu.make_async_copy(f_in, FR, local_sem.at[0])
    own_v = pltpu.make_async_copy(v_in, VR, local_sem.at[1])
    own_v.start()
    own_f.start()

    barrier = pltpu.get_barrier_semaphore()
    has = {k: jnp.logical_and(d + k >= 0, d + k < D) for k in (-2, -1, 1, 2)}
    expected = G - 1
    for j in range(1, G):
        pl.semaphore_signal(barrier, inc=1, device_id=(lax.rem(g + j, G), d), device_id_type=MESH)
    for k in (-2, -1, 1, 2):
        @pl.when(has[k])
        def _(k=k):
            pl.semaphore_signal(barrier, inc=1, device_id=(g, d + k), device_id_type=MESH)
        expected = expected + has[k].astype(jnp.int32)

    @pl.when(d == 0)
    def _():
        RV[:, 0:HV] = jnp.zeros((G, HV, xl, Z), f32)
        RF[:, :, 0:HF] = jnp.zeros((G, 4, HF, xl, Z), f32)
        U0b[:, 0:2] = jnp.zeros((4, 2, X, Z), f32)
        EPr[0] = jnp.zeros((2, X, Z), f32)
        QBr[0] = jnp.zeros((2, 2, X, Z), f32)
        QYr[0] = jnp.zeros((2, 2, X, Z), f32)
        QZr[1] = jnp.zeros((X, Z), f32)

    @pl.when(d < 2)
    def _():
        EP2r[0] = jnp.zeros((X, Z), f32)
        QZr[0] = jnp.zeros((X, Z), f32)

    @pl.when(d == D - 1)
    def _():
        RV[:, HV + yl:] = jnp.zeros((G, HV, xl, Z), f32)
        RF[:, :, HF + yl:] = jnp.zeros((G, 4, HF, xl, Z), f32)
        U0b[:, yl + 4:] = jnp.zeros((4, 2, X, Z), f32)
        EPr[1] = jnp.zeros((2, X, Z), f32)
        QBr[1] = jnp.zeros((2, 2, X, Z), f32)
        QYr[1] = jnp.zeros((2, 2, X, Z), f32)
        QZr[2] = jnp.zeros((X, Z), f32)

    @pl.when(d >= D - 2)
    def _():
        EP2r[1] = jnp.zeros((X, Z), f32)
        QZr[3] = jnp.zeros((X, Z), f32)

    def planes(c, y, h):
        start = c * xl * yl * (Z // 128) + (y // 8) * 8 * (Z // 128) + h * 8 + y % 8
        return pl.ds(start, xl, stride=yl * (Z // 128))

    own_v.wait()
    for y in range(yl):
        for h in range(Z // 128):
            RV[g, HV + y, :, h * 128:(h + 1) * 128] = VR[planes(0, y, h), :]
    own_f.wait()
    for c in range(4):
        for y in range(yl):
            for h in range(Z // 128):
                RF[g, c, HF + y, :, h * 128:(h + 1) * 128] = FR[planes(c, y, h), :]

    pl.semaphore_wait(barrier, expected)

    def rdma(src, dst, ss, rs, target):
        return pltpu.make_async_remote_copy(
            src_ref=src, dst_ref=dst, send_sem=ss, recv_sem=rs,
            device_id=target, device_id_type=MESH)

    halo = ((1, (2, 3)), (-1, (4, 5)))

    def first(j, slot, source):
        other = lax.rem(g + j, G)
        at = other if source else g
        k = (0, 0, 1, 1, -1, -1)[slot]
        width = HF if slot % 2 else HV
        put = {0: width, 1: 0, -1: width + yl}[k]
        count = yl if k == 0 else width
        rows = put if j else {1: yl, -1: width}[k]
        if slot % 2:
            src, dst = RF.at[g, :, pl.ds(rows, count)], RF.at[at, :, pl.ds(put, count)]
        else:
            src, dst = RV.at[g, pl.ds(rows, count)], RV.at[at, pl.ds(put, count)]
        target = (other, d) if j else (g, d + k)
        return rdma(src, dst, s1.at[j, slot], r1.at[at, slot], target)

    for k, slots in halo:
        @pl.when(has[k])
        def _(slots=slots):
            for slot in slots:
                first(0, slot, False).start()
    for slot in (0, 1):
        for j in range(1, G):
            first(j, slot, False).start()

    lo1, hi1 = H1, H1 + n1
    later = {
        "e_up": (EPs.at[1], EPr.at[0], 1),
        "e_down": (EPs.at[0], EPr.at[1], -1),
        "e_up2": (EPs.at[1, 0], EP2r.at[0], 2),
        "e_down2": (EPs.at[0, 0], EP2r.at[1], -2),
        "b_up": (QBs.at[1], QBr.at[0], 1),
        "b_down": (QBs.at[0], QBr.at[1], -1),
        "x_up": (U0b.at[:, pl.ds(yl, 2)], U0b.at[:, pl.ds(0, 2)], 1),
        "x_down": (U0b.at[:, pl.ds(4, 2)], U0b.at[:, pl.ds(yl + 4, 2)], -1),
        "y_up": (QYs.at[1], QYr.at[0], 1),
        "y_down": (QYs.at[0], QYr.at[1], -1),
        "z_up2": (QZs, QZr.at[0], 2),
        "z_up": (QZs, QZr.at[1], 1),
        "z_down": (QZs, QZr.at[2], -1),
        "z_down2": (QZs, QZr.at[3], -2),
    }
    index_of = {name: i for i, name in enumerate(later)}

    def copy_of(name):
        src, dst, k = later[name]
        i = index_of[name]
        return rdma(src, dst, s2.at[i], r2.at[i], (g, d + k)), k

    def start(*names):
        for name in names:
            copy, k = copy_of(name)
            pl.when(has[k])(copy.start)

    def receive(*names):
        for name in names:
            copy, k = copy_of(name)
            pl.when(has[-k])(copy.wait_recv)

    def sent(*names):
        for name in names:
            copy, k = copy_of(name)
            pl.when(has[k])(copy.wait_send)

    sub = lax.broadcasted_iota(jnp.int32, (X, Z), 0)
    lane = lax.broadcasted_iota(jnp.int32, (X, Z), 1)

    def roll(value, shift, dim):
        axis = value.ndim - 2 + dim
        return pltpu.roll(value, shift % value.shape[axis], axis)

    def partner(value, s):
        value = value + jnp.where((sub & s) == 0, roll(value, -s, 0), roll(value, s, 0))
        return value + jnp.where((lane & s) == 0, roll(value, -s, 1), roll(value, s, 1))

    def spread(value, ids, dim, s):
        odd = (ids & s) != 0
        return (jnp.where(odd, roll(value, s, dim), value),
                jnp.where(odd, value, roll(value, -s, dim)))

    def pack2(c):
        return jnp.where((lane & 1) != 0, c[1], c[0])

    def unpack2(packed):
        return spread(packed, lane, 1, 1)

    def pick4(c, ids):
        a, b = (ids & 1) != 0, (ids & 2) != 0
        return jnp.where(b, jnp.where(a, c[3], c[2]), jnp.where(a, c[1], c[0]))

    def spread4(packed, ids, dim):
        even, odd = spread(packed, ids, dim, 1)
        v0, v2 = spread(even, ids, dim, 2)
        v1, v3 = spread(odd, ids, dim, 2)
        return [v0, v1, v2, v3]

    def next_of(get, i, s, last):
        if s == 1:
            return get(i + 1)
        return jnp.where((sub & (s - 1)) == s - 1,
                         roll(get(min(i + 1, last)), s - 1, 0), roll(get(i), -1, 0))

    def prev_of(get, i, s, last):
        if s == 1:
            return get(i - 1)
        return jnp.where((sub & (s - 1)) == 0,
                         roll(get(max(i - 1, 0)), 1 - s, 0), roll(get(i), 1, 0))

    def level(s, E, B, C):
        last = E.shape[0] - 1
        inside = ((sub < X - s), (sub >= s), (lane < Z - s), (lane >= s))
        half = [jnp.where(m, f32(0.5 / s), f32(0.0)) for m in inside]
        scale = 1.0 / (s * s)

        def coefficients(lo, hi):
            def body(r):
                e = E[r]
                xs = [jnp.where(m, roll(e, sh, dim), 0.0)
                      for m, sh, dim in zip(inside, (-s, s, -s, s), (0, 0, 1, 1))]
                get = lambda i: E[i]
                ys = [next_of(get, r, s, last), prev_of(get, r, s, last)]
                fx = [(e + other) * (0.5 * scale) for other in xs]
                fy = [(e + other) * (0.5 * scale) for other in ys]
                diagonal = (fx[0] + fx[1]) + (fy[0] + fy[1]) + (fx[2] + fx[3])
                for i in range(4):
                    C[i, r] = jnp.where(inside[i], fx[i], 0.0)
                C[4, r] = fy[0]
                C[5, r] = fy[1]
                real = e > 0.0
                C[6, r] = jnp.where(real, OMEGA / jnp.where(real, diagonal, 1.0), 0.0)
                C[7, r] = BETA * e
                C[8, r] = diagonal
            over(lo, hi, body)

        def begin(U, lo, hi):
            def body(r):
                w = C[6, r]
                for c in range(3):
                    U[c, r] = w * B[c, r]
                U[3, r] = C[7, r] * B[3, r]
            over(lo, hi, body)

        def parts(U, r):
            coef = [C[i, r] for i in range(6)]
            centre = [U[c, r] for c in range(4)]
            rolled = []
            for c in range(4):
                u = centre[c]
                rolled.append([roll(u, -s, 0), roll(u, s, 0), roll(u, -s, 1), roll(u, s, 1),
                               next_of(lambda i: U[c, i], r, s, last),
                               prev_of(lambda i: U[c, i], r, s, last)])
            p = rolled[3]
            grad = [half[0] * p[0] - half[1] * p[1], (p[4] - p[5]) * (0.5 / s),
                    half[2] * p[2] - half[3] * p[3]]
            out = []
            for c in range(3):
                t = [coef[i] * rolled[c][i] for i in range(6)]
                total = (t[0] + t[1]) + (t[2] + t[3]) + (t[4] + t[5])
                out.append((B[c, r] - grad[c]) + total)
            div = ((half[0] * rolled[0][0] - half[1] * rolled[0][1])
                   + (rolled[1][4] - rolled[1][5]) * (0.5 / s)
                   + (half[2] * rolled[2][2] - half[3] * rolled[2][3]))
            out.append(B[3, r] - div)
            return centre, out

        def sweep(U, V, lo, hi, also=None):
            def body(r):
                centre, out = parts(U, r)
                w = C[6, r]
                for c in range(3):
                    V[c, r] = (1.0 - OMEGA) * centre[c] + w * out[c]
                V[3, r] = centre[3] + C[7, r] * out[3]
            over(lo, hi, body)

        def residual(U, r):
            centre, out = parts(U, r)
            diagonal = C[8, r]
            return [out[c] - diagonal * centre[c] for c in range(3)] + [out[3]]

        return coefficients, begin, sweep, residual

    def restrict0(rows):
        return jnp.where((sub & 1) == 0, partner(rows[0] + rows[1], 1),
                         partner(rows[2] + rows[3], 1)) * 0.125

    def restrict1(tile):
        tile = tile + jnp.where((sub & 1) == 0, roll(tile, -1, 0), roll(tile, 1, 0))
        return partner(tile, 2) * 0.125

    coef0, begin0, sweep0, res0 = level(1, E0, B0, C0)
    coef1, begin1, sweep1, res1 = level(2, E1, B1, C1)
    coef2, begin2, sweep2, res2 = level(4, E2, B2, C2)

    def place_v(lo, hi):
        for i in range(G):
            E0[lo:hi, i * xl:(i + 1) * xl, :] = RV[i, lo:hi]

    def place_f(lo, hi):
        for i in range(G):
            for c in range(4):
                B0[c, lo + H0 - HF:hi + H0 - HF, i * xl:(i + 1) * xl, :] = RF[i, c, lo:hi]

    def hand_on():
        for k, slots in halo:
            @pl.when(has[-k])
            def _(slots=slots):
                for slot in slots:
                    first(0, slot, True).wait_recv()
                    for j in range(1, G):
                        first(j, slot, False).start()

    for j in range(1, G):
        first(j, 0, True).wait_recv()
    place_v(HV, HV + yl)

    def coarse_e(r):
        E1[lo1 + r] = restrict0([E0[H0 + 4 * r + i] for i in range(4)])
    over(0, n1, coarse_e)
    packed = pick4([restrict1(E1[lo1 + i]) for i in range(n1)], sub)
    E2[NEAR] = packed
    EPs[0, 0] = packed
    EPs[1, 0] = packed
    EPs[0, 1] = pack2([E1[lo1], E1[lo1 + 1]])
    EPs[1, 1] = pack2([E1[hi1 - 2], E1[hi1 - 1]])
    start("e_up", "e_down", "e_up2", "e_down2")

    for j in range(1, G):
        first(j, 1, True).wait_recv()
    place_f(HF, HF + yl)
    top, end = H0, H0 + yl
    coef0(top + 1, end - 1)
    begin0(U0a, top + 1, end - 1)
    hand_on()
    sweep0(U0a, U0b, top + 2, end - 2)

    for k, slots in halo:
        @pl.when(has[-k])
        def _(slots=slots):
            for slot in slots:
                for j in range(1, G):
                    first(j, slot, True).wait_recv()
    for a, b in ((0, HV), (HV + yl, 2 * HV + yl)):
        place_v(a, b)
    for a, b in ((0, HF), (HF + yl, 2 * HF + yl)):
        place_f(a, b)
    for a, b in ((top - 2, top + 1), (end - 1, end + 2)):
        coef0(a, b)
        begin0(U0a, a, b)
    for a, b in ((top - 1, top + 2), (end - 2, end + 1)):
        sweep0(U0a, U0b, a, b)

    def coarse_b(r):
        rows = [res0(U0b, H0 + 4 * r + i) for i in range(4)]
        for c in range(4):
            B1[c, lo1 + r] = restrict0([row[c] for row in rows])
    over(0, n1, coarse_b, 2)

    def pack_tiles(packed, U):
        for i in range(2):
            for half in range(2):
                pair = (2 * half, 2 * half + 1)
                packed[0, i, half] = pack2([U[c, lo1 + i] for c in pair])
                packed[1, i, half] = pack2([U[c, hi1 - 2 + i] for c in pair])

    def unpack_tiles(packed, U):
        for i in range(2):
            for half in range(2):
                for side, at in ((0, lo1 - 2), (1, hi1)):
                    for c, value in enumerate(unpack2(packed[side, i, half])):
                        U[2 * half + c, at + i] = value

    pack_tiles(QBs, B1)
    start("b_up", "b_down")

    receive("e_up", "e_down", "e_up2", "e_down2")
    for i in range(2):
        E1[i] = unpack2(EPr[0, 1])[i]
        E1[hi1 + i] = unpack2(EPr[1, 1])[i]
    for at, value in ((0, EP2r[0]), (1, EPr[0, 0]), (3, EPr[1, 0]), (4, EP2r[1])):
        E2[at] = value
    coef1(0, hi1 + 2)
    coef2(0, 2 * NEAR + 1)
    begin1(U1a, lo1, hi1)
    receive("b_up", "b_down")
    unpack_tiles(QBr, B1)
    begin1(U1a, lo1 - 2, lo1)
    begin1(U1a, hi1, hi1 + 2)
    sweep1(U1a, U1b, lo1 - 1, hi1 + 1)
    rows = []
    for i in range(n1):
        rows.append([restrict1(value) for value in res1(U1b, lo1 + i)])
    for c in range(4):
        B2[c, NEAR] = pick4([row[c] for row in rows], sub)
    QZs[...] = pick4([B2[c, NEAR] for c in range(4)], lane)
    start("z_up2", "z_down2", "z_up", "z_down")
    pack_tiles(QYs, U1b)
    start("y_up", "y_down", "x_up", "x_down")

    begin2(U2a, NEAR, NEAR + 1)
    receive("z_up2", "z_up", "z_down", "z_down2")
    for slot, at in enumerate((0, 1, 3, 4)):
        for c, field in enumerate(spread4(QZr[slot], lane, 1)):
            B2[c, at] = field
    begin2(U2a, 0, NEAR)
    begin2(U2a, NEAR + 1, 2 * NEAR + 1)
    here, there = U2a, U2b
    for i in range(COARSE - 1):
        sweep2(here, there, 0, 2 * NEAR + 1)
        here, there = there, here

    receive("y_up", "y_down")
    unpack_tiles(QYr, U1b)
    for c in range(4):
        below, own, above = [spread4(here[c, i], sub, 0) for i in (1, 2, 3)]
        for i, z in enumerate(below[2:] + own + above[:2]):
            U1b[c, i] = U1b[c, i] + z
    sweep1(U1b, U1a, 0, hi1 + 2)
    sweep1(U1a, U1b, lo1 - 1, hi1 + 1)

    receive("x_up", "x_down")
    sent("x_up", "x_down")

    def add0(r):
        for c in range(4):
            for i, y in enumerate(spread(U1b[c, lo1 + r], sub, 0, 1)):
                for at in (H0 + 4 * r + 2 * i, H0 + 4 * r + 2 * i + 1):
                    U0b[c, at] = U0b[c, at] + y
    over(0, n1, add0, 2)
    for c in range(4):
        low = spread(U1b[c, lo1 - 1], sub, 0, 1)
        high = spread(U1b[c, hi1], sub, 0, 1)
        for at, y in ((0, low[0]), (1, low[1]), (2, low[1]),
                      (yl + 3, high[0]), (yl + 4, high[0]), (yl + 5, high[1])):
            U0b[c, at] = U0b[c, at] + y
    sweep0(U0b, U0a, top - 2, end + 2)
    sweep0(U0a, U0b, top - 1, end + 1)

    def own_planes(value):
        kept = value[:xl]
        for i in range(1, G):
            kept = jnp.where(g == i, value[i * xl:(i + 1) * xl], kept)
        return kept

    def store(ref, c, r, value):
        kept = own_planes(value)
        for h in range(Z // 128):
            ref[planes(c, r, h), :] = kept[:, h * 128:(h + 1) * 128]

    def finish_x(r):
        for c in range(4):
            store(XO, c, r, U0b[c, H0 + r])
    over(0, yl, finish_x)
    put_x = pltpu.make_async_copy(XO, x_out, local_sem.at[2])
    put_x.start()

    def finish_r(r):
        for c, value in enumerate(res0(U0b, H0 + r)):
            store(RO, c, r, value)
    over(0, yl, finish_r)
    put_r = pltpu.make_async_copy(RO, r_out, local_sem.at[3])
    put_r.start()

    for k, slots in halo:
        @pl.when(has[k])
        def _(slots=slots):
            for slot in slots:
                first(0, slot, False).wait_send()

        @pl.when(has[-k])
        def _(slots=slots):
            for slot in slots:
                for j in range(1, G):
                    first(j, slot, False).wait_send()
    for slot in (0, 1):
        for j in range(1, G):
            first(j, slot, False).wait_send()
    sent(*[name for name in later if not name.startswith("x_")])
    put_x.wait()
    put_r.wait()


def write_out(x_in, r_in, x_out, r_out, held, sems):
    half = x_in.shape[0] // 2
    chunks = [(a.at[pl.ds(i * half, half)], b.at[pl.ds(i * half, half)])
              for a, b in ((x_in, x_out), (r_in, r_out)) for i in range(2)]
    into = [pltpu.make_async_copy(a, held.at[i], sems.at[0, i]) for i, (a, _) in enumerate(chunks)]
    back = [pltpu.make_async_copy(held.at[i], b, sems.at[1, i]) for i, (_, b) in enumerate(chunks)]
    for copy in into:
        copy.start()
    for arrived, copy in zip(into, back):
        arrived.wait()
        copy.start()
    for copy in back:
        copy.wait()


def tiles(array):
    Z = array.shape[-1]
    return jnp.swapaxes(array.reshape(-1, 8, Z // 128, 128), 1, 2).reshape(-1, 128)


def local(G, D, forcing, viscosity):
    _, xl, yl, Z = forcing.shape
    X = G * xl
    assert yl == 16 and xl % 4 == 0 and D > NEAR
    rows0, rows1, rows2 = yl + 2 * H0, yl // 4 + 2 * H1, 1 + 2 * NEAR
    f32 = jnp.float32
    vm = lambda *shape: pltpu.VMEM(shape, f32)
    sem = pltpu.SemaphoreType.DMA
    out = jax.ShapeDtypeStruct((4 * xl * yl * (Z // 128), 128), f32)
    field = lambda rows: vm(4, rows, X, Z)
    hbm_spec = pl.BlockSpec(memory_space=pltpu.HBM)
    solved, left = pl.pallas_call(
        functools.partial(kernel, G, D, yl, xl, Z),
        out_shape=(out, out),
        in_specs=[hbm_spec, hbm_spec],
        out_specs=(hbm_spec, hbm_spec),
        scratch_shapes=[
            *[vm(4 * xl * yl * (Z // 128), 128)] * 3, vm(xl * yl * (Z // 128), 128),
            vm(G, 4, yl + 2 * HF, xl, Z), vm(G, yl + 2 * HV, xl, Z),
            vm(rows0, X, Z), field(rows0), field(rows0), field(rows0), vm(9, rows0, X, Z),
            vm(rows1, X, Z), field(rows1), field(rows1), field(rows1), vm(9, rows1, X, Z),
            vm(rows2, X, Z), field(rows2), field(rows2), field(rows2), vm(9, rows2, X, Z),
            vm(2, 2, X, Z), vm(2, 2, X, Z), vm(2, X, Z),
            vm(2, 2, 2, X, Z), vm(2, 2, 2, X, Z),
            vm(2, 2, 2, X, Z), vm(2, 2, 2, X, Z),
            vm(X, Z), vm(4, X, Z),
            sem((4,)), sem((G, 6)), sem((G, 6)), sem((14,)), sem((14,)),
        ],
        compiler_params=pltpu.CompilerParams(
            collective_id=0, has_side_effects=True, vmem_limit_bytes=GRANT),
    )(tiles(forcing), tiles(viscosity))
    solved, left = pl.pallas_call(
        write_out,
        out_shape=(out, out),
        in_specs=[hbm_spec, hbm_spec],
        out_specs=(hbm_spec, hbm_spec),
        scratch_shapes=[vm(4, 2 * xl * yl * (Z // 128), 128), sem((2, 4))],
        compiler_params=pltpu.CompilerParams(vmem_limit_bytes=GRANT),
    )(solved, left)

    def whole(array):
        array = array.reshape(4 * xl * yl // 8, Z // 128, 8, 128)
        return jnp.swapaxes(array, 1, 2).reshape(forcing.shape)

    return whole(solved), whole(left)


def solution(mesh):
    G, D = mesh.shape["grp"], mesh.shape["dev"]
    in_specs = (P(None, "grp", "dev", None), P("grp", "dev", None))
    out_specs = (P(None, "grp", "dev", None), P(None, "grp", "dev", None))
    return jax.shard_map(
        functools.partial(local, G, D), mesh=mesh, in_specs=in_specs, out_specs=out_specs,
        check_vma=False)
```
